32 devices in a mesh: dp: 4 (over x, core), fsdp: 8 (over z, y).
Axes of the slice: x: 2, y: 2, z: 4, core: 2. Of those that a mesh axis runs over, the one named last changes fastest.
Arguments:
- hidden_input: bfloat16 [4, 2, 1024, 8192], P('dp', None, 'fsdp'), may hold values from -6 to 6
- readout: bfloat16 [4, 2, 1024, 512], P('dp', None, 'fsdp'), may hold values from -0.26367188 to 0.26367188
- response: int32 [4, 2, 1024], P('dp', None, 'fsdp'), may hold values from 0 to 1, as said below
- value_matrix: bfloat16 [8192, 512], P('fsdp'), may hold values from -0.0625 to 0.0625
- adapter_down: bfloat16 [8192, 64], P('fsdp'), may hold values from -0.0625 to 0.0625
- adapter_up: bfloat16 [64, 512], replicated, may hold values from -0.037353516 to 0.037353516
Outputs:
- down_gradient: float32 [8192, 64], P('fsdp')
- grad_b_t: float32 [512, 64], P('fsdp')
- losses: float32 [4], P('dp')
- margins: float32 [4], P('dp')
The draws below stay inside these ranges and needn't reach their ends.
Inputs may be any that keep to these rules, and one draw needn't show every extreme that they name: `response`: each sequence's 1s form one contiguous run of tokens that starts between 128 and 512 and ends between 768 and 1024.
All inputs are finite; a program needn't handle non-finite values.
Results may differ from the reference program's by a relative error of at most 0.0055.
Values may be sent and summed in bfloat16 or wider, within the bound.
A program may use at most 64 MiB of HBM per device.

```python
import jax
import jax.numpy as jnp
from jax import lax

MODEL_WIDTH = 8192
VALUE_FEATURES = 512
ADAPTER_RANK = 64
LEN = 1024
PAIRS = 4


def draw_response(key, part):
    key = jax.random.fold_in(key, 7)
    first_key, second_key = jax.random.split(key)
    starts = jax.random.randint(first_key, (PAIRS, 2, 1), LEN // 8, LEN // 2 + 1)
    finish = jax.random.randint(second_key, (PAIRS, 2, 1), 3 * LEN // 4, LEN + 1)
    places = jnp.arange(LEN, dtype=jnp.int32)[None, None, :]
    inside = jnp.logical_and(places >= starts, places < finish)
    return inside.astype(jnp.int32)


def steps_of(own_key, dims, cuts, low, high):
    level = 1.0
    for axis_at, shards_of in cuts:
        steps = jax.random.uniform(jax.random.fold_in(jax.random.fold_in(own_key, 6), axis_at), (shards_of,), jnp.float32, low / len(cuts), high / len(cuts))
        level = level * jnp.repeat(jnp.exp(steps), dims[axis_at] // shards_of).reshape((-1,) + (1,) * (len(dims) - 1 - axis_at))
    return level


def bell_draw(stream_key, shape, deviation, reach, cuts=(), kind=jnp.bfloat16):
    gain = steps_of(stream_key, shape, cuts, -0.22, 0.18) if cuts else 1.0
    values = jax.random.normal(stream_key, shape, jnp.float32) * deviation * gain
    return jnp.minimum(jnp.maximum(values, -reach), reach).astype(kind)


def setup_inputs(seed: int = 0) -> dict:
    key_list = jax.random.split(jax.random.key(seed), 7)
    hidden_input = bell_draw(key_list[0], (PAIRS, 2, LEN, MODEL_WIDTH), 1.0, 6.0, ((0, 4), (2, 8)))
    readout = bell_draw(key_list[1], (PAIRS, 2, LEN, VALUE_FEATURES), (1.0 / VALUE_FEATURES ** 0.5), 0.26367188, ((0, 4), (2, 8)))
    response = draw_response(jax.random.fold_in(key_list[6], 71), 0)
    value_matrix = bell_draw(key_list[3], (MODEL_WIDTH, VALUE_FEATURES), MODEL_WIDTH ** -0.5, 0.0625, ((0, 8),))
    adapter_down = bell_draw(key_list[4], (MODEL_WIDTH, ADAPTER_RANK), MODEL_WIDTH ** -0.5, 0.0625, ((0, 8),))
    adapter_up = bell_draw(key_list[5], (ADAPTER_RANK, VALUE_FEATURES), (0.05 / ADAPTER_RANK ** 0.5), 0.037353516)
    return {"hidden_input": hidden_input, "readout": readout, "response": response, "value_matrix": value_matrix, "adapter_down": adapter_down, "adapter_up": adapter_up}


DPO_BETA = 0.5
ADAPTER_SCALE = 2.0


def pairwise_terms(token_pair, pair_readout, pair_mask, value_matrix, adapter_down, adapter_up):
    seq_total = token_pair.shape[1]
    token_row_block = token_pair.reshape(2 * seq_total, token_pair.shape[2])
    base_output = jnp.dot(token_row_block, value_matrix, preferred_element_type=jnp.float32)
    lowrank_output = jnp.dot(token_row_block, adapter_down, preferred_element_type=jnp.float32).astype(jnp.bfloat16)
    policy_score = base_output + ADAPTER_SCALE * jnp.dot(lowrank_output, adapter_up, preferred_element_type=jnp.float32)
    read_f = pair_readout.reshape(2 * seq_total, -1).astype(jnp.float32)
    mask_f = pair_mask.reshape(2 * seq_total).astype(jnp.float32)
    t_pol = jnp.tanh(policy_score)
    t_ref = jnp.tanh(base_output)
    scores = jnp.sum(read_f * (t_pol - t_ref), axis=1) * mask_f
    ratio = jnp.sum(scores.reshape(2, seq_total), axis=1)
    reward_margin = DPO_BETA * (ratio[0] - ratio[1])
    pair_loss_total = jax.nn.softplus(-reward_margin)
    gate = jax.nn.sigmoid(-reward_margin)
    coef = DPO_BETA * gate * jnp.array([-1.0, 1.0], jnp.float32)
    coef_rows = jnp.repeat(coef, seq_total)
    hidden_gradient = (coef_rows[:, None] * mask_f[:, None] * read_f * (1.0 - t_pol * t_pol)).astype(jnp.bfloat16)
    up_gradient_flipped = ADAPTER_SCALE * lax.dot_general(hidden_gradient, lowrank_output, (((0,), (0,)), ((), ())), preferred_element_type=jnp.float32)
    lowrank_gradient = (ADAPTER_SCALE * lax.dot_general(hidden_gradient, adapter_up, (((1,), (1,)), ((), ())), preferred_element_type=jnp.float32)).astype(jnp.bfloat16)
    down_gradient = lax.dot_general(token_row_block, lowrank_gradient, (((0,), (0,)), ((), ())), preferred_element_type=jnp.float32)
    return down_gradient, up_gradient_flipped, pair_loss_total, reward_margin


def reference(hidden_input, readout, response, value_matrix, adapter_down, adapter_up):
    def step(totals, items):
        token_pair, pair_readout, pair_mask = items
        down_gradient, up_gradient_flipped, pair_loss_total, reward_margin = pairwise_terms(token_pair, pair_readout, pair_mask, value_matrix, adapter_down, adapter_up)
        return (totals[0] + down_gradient, totals[1] + up_gradient_flipped), (pair_loss_total, reward_margin)

    start_sums = (jnp.zeros((MODEL_WIDTH, ADAPTER_RANK), jnp.float32), jnp.zeros((VALUE_FEATURES, ADAPTER_RANK), jnp.float32))
    sums, outs = lax.scan(step, start_sums, (hidden_input, readout, response))
    return sums[0], sums[1], outs[0], outs[1]
```

```python
import functools

import jax
import jax.numpy as jnp
from jax import lax
from jax.experimental import pallas as pl
from jax.experimental.pallas import tpu as pltpu
from jax.sharding import PartitionSpec as P

DPO_BETA = 0.5
ADAPTER_SCALE = 2.0
LANES = 128
PACK = 128
PIECES = 6
MESH = pl.DeviceIdType.MESH


def kernel(
    n_dp, n_fsdp,
    hid_hbm, read_hbm, resp_ref, value_hbm, down_ref, up_ref,
    down_out, up_out, loss_out, margin_out,
    hid, read, weights, base, acc_l, acc_r, t_pol, grad_low_t,
    ratio_buf, part, buf1, send2, buf2, total2, send3, buf3, final,
    local_sem, ring_s, ring_r, x_s, x_r, core_s, core_r,
    ratio_s, ratio_r, s1, r1, s2, r2, s3, r3, s4, r4,
):
    half = n_fsdp // 2
    rows = value_hbm.shape[0]
    rank = down_ref.shape[1]
    tokens = hid.shape[0]
    seq = tokens // 2
    piece_rows = weights.shape[1] // PIECES
    groups = rows // PACK
    up_rows = base.shape[1] // n_fsdp

    me = lax.axis_index("fsdp")
    d = lax.axis_index("dp")
    core = lax.rem(d, 2)
    xbit = lax.rem(lax.div(d, 2), 2)
    core_peer = d + 1 - 2 * core
    x_peer = d + 2 - 4 * xbit

    col, row = lax.rem(me, 2), lax.div(me, 2)
    pos = row * (1 - col) + (n_fsdp - 1 - row) * col

    def at(p):
        p = lax.rem(p + 2 * n_fsdp, n_fsdp)
        c = lax.div(p, half)
        r = p * (1 - c) + (n_fsdp - 1 - p) * c
        return 2 * r + c

    ring_peer = (at(pos + 1), at(pos - 1))

    def shard_of(way, s):
        return at(pos - s) if way == 0 else at(pos + s)

    def piece(q, p):
        return weights.at[q, pl.ds(pl.multiple_of(p * piece_rows, piece_rows), piece_rows), :]

    own = (xbit * 2 + core, 4 + core)
    x_own = (1 - xbit) * 2 + core
    core_own = (xbit * 2 + 1 - core, 4 + 1 - core, (1 - xbit) * 2 + 1 - core)

    def remote(src, dst, send, recv, **where):
        return pltpu.make_async_remote_copy(
            src_ref=src, dst_ref=dst, send_sem=send, recv_sem=recv,
            device_id=where, device_id_type=MESH,
        )

    def ring_copy(way, s, kind, q):
        ref = piece(q, own[kind])
        return remote(ref, ref, ring_s.at[way, s - 1, kind], ring_r.at[way, s - 1, kind], fsdp=ring_peer[way])

    def x_copy(way, s, q, p):
        ref = piece(q, p)
        return remote(ref, ref, x_s.at[way, s - 1], x_r.at[way, s - 1], dp=x_peer)

    def core_copy(way, s, kind, q, p):
        ref = piece(q, p)
        return remote(ref, ref, core_s.at[way, s - 1, kind], core_r.at[way, s - 1, kind], dp=core_peer)

    def has(way, s, kind):
        return s < half or (s == half and way == kind)

    value_copy = pltpu.make_async_copy(value_hbm, weights.at[me, pl.ds(0, rows), :], local_sem.at[0])
    hid_copy = pltpu.make_async_copy(hid_hbm, hid, local_sem.at[1])
    read_copy = pltpu.make_async_copy(read_hbm, read, local_sem.at[2])
    value_copy.start()
    hid_copy.start()
    read_copy.start()

    barrier = pltpu.get_barrier_semaphore()

    def greet_fsdp(k, _):
        pl.semaphore_signal(barrier, inc=1, device_id={"fsdp": lax.rem(me + k, n_fsdp)}, device_id_type=MESH)
        return 0

    def greet_dp(k, _):
        pl.semaphore_signal(barrier, inc=1, device_id={"dp": lax.rem(d + k, n_dp)}, device_id_type=MESH)
        return 0

    lax.fori_loop(1, n_fsdp, greet_fsdp, 0)
    lax.fori_loop(1, n_dp, greet_dp, 0)

    packed = [down_ref[g * PACK:(g + 1) * PACK, :] for g in range(groups)]
    width = weights.shape[2]
    if groups * rank < width:
        packed.append(jnp.zeros((PACK, width - groups * rank), jnp.bfloat16))
    weights[me, pl.ds(rows, PACK), :] = jnp.concatenate(packed, axis=1)

    value_copy.wait()
    pl.semaphore_wait(barrier, n_fsdp + n_dp - 2)

    for kind in (0, 1):
        for way in (0, 1):
            if has(way, 1, kind):
                ring_copy(way, 1, kind, me).start()

    def multiply(q):
        first = pl.multiple_of(q * rows, rows)
        base[...] += jnp.dot(
            hid[:, pl.ds(first, rows)], weights[q, 0:rows, :], preferred_element_type=jnp.float32
        )
        left, right = acc_l[...], acc_r[...]
        for t in range(groups // 2):
            tile = weights[q, rows:rows + PACK, t * LANES:(t + 1) * LANES]
            begin = pl.multiple_of(q * rows + 2 * t * PACK, PACK)
            left += jnp.dot(hid[:, pl.ds(begin, PACK)], tile, preferred_element_type=jnp.float32)
            begin = pl.multiple_of(q * rows + (2 * t + 1) * PACK, PACK)
            right += jnp.dot(hid[:, pl.ds(begin, PACK)], tile, preferred_element_type=jnp.float32)
        acc_l[...] = left
        acc_r[...] = right

    base[...] = jnp.zeros_like(base)
    acc_l[...] = jnp.zeros_like(acc_l)
    acc_r[...] = jnp.zeros_like(acc_r)
    hid_copy.wait()
    multiply(me)

    def take_ring(s, kind):
        for way in (0, 1):
            if has(way, s, kind):
                q = shard_of(way, s)
                ring_copy(way, s, kind, q).wait_recv()
                if has(way, s + 1, kind):
                    ring_copy(way, s + 1, kind, q).start()
                if kind == 0:
                    x_copy(way, s, q, own[0]).start()
                core_copy(way, s, kind, q, own[kind]).start()

    def take_x(s):
        for way in (0, 1):
            if has(way, s, 0):
                q = shard_of(way, s)
                x_copy(way, s, q, x_own).wait_recv()
                core_copy(way, s, 2, q, x_own).start()

    def finish(s):
        for way in (0, 1):
            for kind in (0, 1, 2):
                if has(way, s, kind % 2):
                    core_copy(way, s, kind, shard_of(way, s), core_own[kind]).wait_recv()
        if s == half:
            multiply(shard_of(0, s))
        else:
            def both(i, _):
                multiply(at(pos + s * (2 * i - 1)))
                return 0
            lax.fori_loop(0, 2, both, 0)

    for s in range(1, half + 1):
        take_ring(s, 0)
        if s > 1:
            take_x(s - 1)
        take_ring(s, 1)
        if s > 1:
            finish(s - 1)
    take_x(half)
    finish(half)

    low = (acc_l[:, 0:rank] + acc_r[:, rank:2 * rank]).astype(jnp.bfloat16)
    ref_act = base[...]
    policy = ref_act + ADAPTER_SCALE * jnp.dot(low, up_ref[...], preferred_element_type=jnp.float32)
    t_policy = jnp.tanh(policy)
    t_pol[...] = t_policy
    read_copy.wait()
    resp = resp_ref[...].astype(jnp.float32)
    masks = [
        jnp.transpose(jnp.broadcast_to(resp[i:i + 1, :], (seq, seq)))[:, 0:1] for i in (0, 1)
    ]
    mask = jnp.concatenate(masks, axis=0)
    weighted = read[...].astype(jnp.float32) * mask
    scores = weighted * (t_policy - jnp.tanh(ref_act))
    diff = scores[0:seq, :] - scores[seq:, :]
    tile = jnp.zeros((seq, LANES), jnp.float32)
    for t in range(diff.shape[1] // LANES):
        tile += diff[:, t * LANES:(t + 1) * LANES]
    ratio_buf[me] = jnp.sum(tile.reshape(seq // 8, 8, LANES), axis=0)

    def ratio_copy(k):
        return remote(
            ratio_buf.at[me], ratio_buf.at[me], ratio_s.at[k], ratio_r.at[k], fsdp=lax.rem(me + k, n_fsdp)
        )

    def each(first, last, body):
        def step(k, _):
            body(k)
            return 0
        lax.fori_loop(first, last, step, 0)

    each(1, n_fsdp, lambda k: ratio_copy(k).start())
    base[...] = weighted * (1.0 - t_policy * t_policy)
    each(1, n_fsdp, lambda k: ratio_copy(k).wait())

    margin = DPO_BETA * jnp.sum(jnp.sum(ratio_buf[...], axis=0), keepdims=True)
    loss = jnp.maximum(-margin, 0.0) + jnp.log1p(jnp.exp(-jnp.abs(margin)))
    gate = 1.0 / (1.0 + jnp.exp(margin))
    loss_out[...] = jnp.broadcast_to(loss, loss_out.shape)
    margin_out[...] = jnp.broadcast_to(margin, margin_out.shape)
    coef = DPO_BETA * gate
    grad_h = jnp.concatenate(
        [(-coef * base[0:seq, :]).astype(jnp.bfloat16), (coef * base[seq:, :]).astype(jnp.bfloat16)], axis=0
    )
    grad_low = ADAPTER_SCALE * lax.dot_general(
        grad_h, up_ref[...], (((1,), (1,)), ((), ())), preferred_element_type=jnp.float32
    )
    grad_low_t[...] = jnp.transpose(grad_low).astype(jnp.bfloat16)
    grad_b_t = ADAPTER_SCALE * lax.dot_general(
        grad_h, low, (((0,), (0,)), ((), ())), preferred_element_type=jnp.float32
    )
    for q in range(n_fsdp):
        block = grad_b_t[q * up_rows:(q + 1) * up_rows, :]
        block = jnp.concatenate([block, jnp.zeros((up_rows, LANES - rank), jnp.float32)], axis=1)
        if up_rows < rank:
            block = jnp.concatenate([block, jnp.zeros((rank - up_rows, LANES), jnp.float32)], axis=0)
        part[q, :, rows:rows + LANES] = block

    half_rows, quarter = rank // 2, rank // 4
    mine1 = pl.multiple_of(core * half_rows, half_rows)
    theirs1 = pl.multiple_of((1 - core) * half_rows, half_rows)

    def block_of(k):
        return lax.rem(me + k, n_fsdp)

    def copy1(k):
        return remote(
            part.at[block_of(k), pl.ds(theirs1, half_rows), :], buf1.at[k], s1.at[k], r1.at[k], dp=core_peer
        )

    def copy2(k):
        return remote(send2.at[k], buf2.at[k], s2.at[k], r2.at[k], dp=x_peer)

    def copy3(k):
        return remote(send3.at[k], buf3.at[k], s3.at[k], r3.at[k], fsdp=block_of(k))

    def stage1(k):
        q = block_of(k)
        part[q, :, 0:rows] = jnp.dot(
            grad_low_t[...], hid[:, pl.ds(pl.multiple_of(q * rows, rows), rows)],
            preferred_element_type=jnp.float32,
        )
        copy1(k).start()

    def stage2(k):
        q = block_of(k)
        copy1(k).wait_recv()
        give = pl.multiple_of((1 - xbit) * quarter, quarter)
        keep = pl.multiple_of(xbit * quarter, quarter)
        send2[k] = (part[q, pl.ds(mine1 + give, quarter), :] + buf1[k, pl.ds(give, quarter), :]).astype(jnp.bfloat16)
        copy2(k).start()
        total2[k] = part[q, pl.ds(mine1 + keep, quarter), :] + buf1[k, pl.ds(keep, quarter), :]

    def stage3(k):
        copy2(k).wait_recv()
        send3[k] = (total2[k] + buf2[k].astype(jnp.float32)).astype(jnp.bfloat16)
        copy3(k).start()

    each(1, n_fsdp, stage1)
    stage1(0)
    each(1, n_fsdp, stage2)
    stage2(0)
    each(1, n_fsdp, stage3)
    copy2(0).wait_recv()
    total2[0] = total2[0] + buf2[0].astype(jnp.float32)

    def stage4(k):
        copy3(k).wait_recv()
        total2[0] = total2[0] + buf3[k].astype(jnp.float32)

    each(1, n_fsdp, stage4)
    final[0] = total2[0]

    def copy4(k):
        return remote(final.at[0], final.at[k], s4.at[k], r4.at[k], dp=lax.rem(d + k, n_dp))

    each(1, n_dp, lambda k: copy4(k).start())

    for s in range(1, half + 1):
        for way in (0, 1):
            for kind in (0, 1):
                if has(way, s, kind):
                    ring_copy(way, s, kind, me).wait_send()
                    core_copy(way, s, kind, me, own[kind]).wait_send()
            if has(way, s, 0):
                x_copy(way, s, me, own[0]).wait_send()
                core_copy(way, s, 2, me, x_own).wait_send()
    each(0, n_fsdp, lambda k: copy1(k).wait_send())
    each(0, n_fsdp, lambda k: copy2(k).wait_send())
    each(1, n_fsdp, lambda k: copy3(k).wait_send())

    each(1, n_dp, lambda k: copy4(k).wait())
    for c in (0, 1):
        for x in (0, 1):
            begin = c * half_rows + x * quarter
            total = jnp.zeros((quarter, rows + LANES), jnp.float32)
            for h in range(n_dp // 4):
                slot = lax.rem(d - (h * 4 + x * 2 + c) + n_dp, n_dp)
                total += final[slot]
            down_out[begin:begin + quarter, :] = total[:, 0:rows]
            up_out[begin:begin + quarter, :] = total[:, rows:rows + LANES]


def shards(n_dp, n_fsdp, hidden_input, readout, response, value_matrix, adapter_down, adapter_up):
    seq = hidden_input.shape[2]
    tokens = 2 * seq
    model = hidden_input.shape[3]
    rows, features = value_matrix.shape
    rank = adapter_down.shape[1]
    half = n_fsdp // 2
    quarter = rank // 4
    wide = rows + LANES
    f32, bf16 = jnp.float32, jnp.bfloat16
    vmem = pl.BlockSpec(memory_space=pltpu.VMEM)
    hbm = pl.BlockSpec(memory_space=pl.ANY)
    dma = pltpu.SemaphoreType.DMA
    outs = pl.pallas_call(
        functools.partial(kernel, n_dp, n_fsdp),
        out_shape=(
            jax.ShapeDtypeStruct((rank, rows), f32),
            jax.ShapeDtypeStruct((rank, LANES), f32),
            jax.ShapeDtypeStruct((8, LANES), f32),
            jax.ShapeDtypeStruct((8, LANES), f32),
        ),
        in_specs=[hbm, hbm, vmem, hbm, vmem, vmem],
        out_specs=(vmem, vmem, vmem, vmem),
        scratch_shapes=[
            pltpu.VMEM((tokens, model), bf16),
            pltpu.VMEM((tokens, features), bf16),
            pltpu.VMEM((n_fsdp, rows + PACK, features), bf16),
            pltpu.VMEM((tokens, features), f32),
            pltpu.VMEM((tokens, LANES), f32),
            pltpu.VMEM((tokens, LANES), f32),
            pltpu.VMEM((tokens, features), f32),
            pltpu.VMEM((rank, tokens), bf16),
            pltpu.VMEM((n_fsdp, 8, LANES), f32),
            pltpu.VMEM((n_fsdp, rank, wide), f32),
            pltpu.VMEM((n_fsdp, rank // 2, wide), f32),
            pltpu.VMEM((n_fsdp, quarter, wide), bf16),
            pltpu.VMEM((n_fsdp, quarter, wide), bf16),
            pltpu.VMEM((n_fsdp, quarter, wide), f32),
            pltpu.VMEM((n_fsdp, quarter, wide), bf16),
            pltpu.VMEM((n_fsdp, quarter, wide), bf16),
            pltpu.VMEM((n_dp, quarter, wide), f32),
            dma((3,)),
            dma((2, half, 2)), dma((2, half, 2)),
            dma((2, half)), dma((2, half)),
            dma((2, half, 3)), dma((2, half, 3)),
            dma((n_fsdp,)), dma((n_fsdp,)),
            dma((n_fsdp,)), dma((n_fsdp,)),
            dma((n_fsdp,)), dma((n_fsdp,)),
            dma((n_fsdp,)), dma((n_fsdp,)),
            dma((n_dp,)), dma((n_dp,)),
        ],
        compiler_params=pltpu.CompilerParams(
            collective_id=0, has_side_effects=True, vmem_limit_bytes=56 << 20
        ),
        name="dpo_adapter_gradient",
    )(
        hidden_input.reshape(tokens, model),
        readout.reshape(tokens, features),
        response.reshape(2, seq),
        value_matrix,
        adapter_down,
        adapter_up,
    )
    down_t, up_block, loss, margin = outs
    return (
        down_t.T,
        up_block[:features // n_fsdp, :rank],
        loss[0, :1],
        margin[0, :1],
    )


def solution(mesh):
    placed = (
        P("dp", None, "fsdp", None),
        P("dp", None, "fsdp", None),
        P("dp", None, "fsdp"),
        P("fsdp", None),
        P("fsdp", None),
        P(),
    )
    return jax.shard_map(
        functools.partial(shards, mesh.shape["dp"], mesh.shape["fsdp"]),
        mesh=mesh,
        in_specs=placed,
        out_specs=(P("fsdp", None), P("fsdp", None), P("dp"), P("dp")),
        check_vma=False,
    )
```

```python
import functools

import jax
import jax.numpy as jnp
from jax import lax
from jax.experimental import pallas as pl
from jax.experimental.pallas import tpu as pltpu
from jax.sharding import PartitionSpec as P

DPO_BETA = 0.5
ADAPTER_SCALE = 2.0
LANES = 128
PACK = 128
MESH = pl.DeviceIdType.MESH


def kernel(
    n_dp, n_fsdp,
    hid_hbm, read_hbm, resp_ref, value_hbm, down_ref, up_ref,
    out,
    hid, read, weights, base, acc_l, acc_r, grad_low_t,
    ratio_buf, part, buf1, send2, buf2, total2, send3, buf3, final,
    local_sem, ring_s, ring_r, x_s, x_r, core_s, core_r,
    ratio_s, ratio_r, s1, r1, s2, r2, s3, r3, s4, r4,
):
    half = n_fsdp // 2
    rows = value_hbm.shape[0]
    rank = down_ref.shape[0]
    tokens = hid.shape[0]
    seq = tokens // 2
    swapped = weights.shape[1] * 11 // 72 // 16 * 16
    kept = (weights.shape[1] - 4 * swapped) // 2
    groups = rows // PACK
    up_rows = base.shape[1] // n_fsdp

    me = lax.axis_index("fsdp")
    d = lax.axis_index("dp")
    core = lax.rem(d, 2)
    xbit = lax.rem(lax.div(d, 2), 2)
    core_peer = d + 1 - 2 * core
    x_peer = d + 2 - 4 * xbit

    col, row = lax.rem(me, 2), lax.div(me, 2)
    pos = row * (1 - col) + (n_fsdp - 1 - row) * col

    def at(p):
        p = lax.rem(p + 2 * n_fsdp, n_fsdp)
        c = lax.div(p, half)
        r = p * (1 - c) + (n_fsdp - 1 - p) * c
        return 2 * r + c

    ring_peer = (at(pos + 1), at(pos - 1))

    def shard_of(way, s):
        return at(pos - s) if way == 0 else at(pos + s)

    def piece(q, kind, p):
        if kind == 1:
            return weights.at[q, pl.ds(pl.multiple_of(4 * swapped + p * kept, 16), kept), :]
        return weights.at[q, pl.ds(pl.multiple_of(p * swapped, 16), swapped), :]

    own = (xbit * 2 + core, core)
    x_own = (1 - xbit) * 2 + core
    core_own = (xbit * 2 + 1 - core, 1 - core, (1 - xbit) * 2 + 1 - core)

    def remote(src, dst, send, recv, **where):
        return pltpu.make_async_remote_copy(
            src_ref=src, dst_ref=dst, send_sem=send, recv_sem=recv,
            device_id=where, device_id_type=MESH,
        )

    def ring_copy(way, s, kind, q):
        ref = piece(q, kind, own[kind])
        return remote(ref, ref, ring_s.at[way, s - 1, kind], ring_r.at[way, s - 1, kind], fsdp=ring_peer[way])

    def x_copy(way, s, q, p):
        ref = piece(q, 0, p)
        return remote(ref, ref, x_s.at[way, s - 1], x_r.at[way, s - 1], dp=x_peer)

    def core_copy(way, s, kind, q, p):
        ref = piece(q, kind, p)
        return remote(ref, ref, core_s.at[way, s - 1, kind], core_r.at[way, s - 1, kind], dp=core_peer)

    def has(way, s, kind):
        return s < half or (s == half and way == kind)

    value_copy = pltpu.make_async_copy(value_hbm, weights.at[me, pl.ds(0, rows), :], local_sem.at[0])
    hid_copy = pltpu.make_async_copy(hid_hbm, hid, local_sem.at[1])
    read_copy = pltpu.make_async_copy(read_hbm, read, local_sem.at[2])
    value_copy.start()
    hid_copy.start()
    read_copy.start()

    barrier = pltpu.get_barrier_semaphore()

    def greet_fsdp(k, _):
        pl.semaphore_signal(barrier, inc=1, device_id={"fsdp": lax.rem(me + k, n_fsdp)}, device_id_type=MESH)
        return 0

    def greet_dp(k, _):
        pl.semaphore_signal(barrier, inc=1, device_id={"dp": lax.rem(d + k, n_dp)}, device_id_type=MESH)
        return 0

    lax.fori_loop(1, n_fsdp, greet_fsdp, 0)
    lax.fori_loop(1, n_dp, greet_dp, 0)

    for t in range(groups // 2):
        pair = [down_ref[:, g * PACK:(g + 1) * PACK].astype(jnp.float32) for g in (2 * t, 2 * t + 1)]
        tile = jnp.transpose(jnp.concatenate(pair, axis=0)).astype(jnp.bfloat16)
        weights[me, rows:rows + PACK, t * LANES:(t + 1) * LANES] = tile
    used = groups // 2 * LANES
    if used < weights.shape[2]:
        weights[me, rows:rows + PACK, used:] = jnp.zeros((PACK, weights.shape[2] - used), jnp.bfloat16)

    value_copy.wait()
    pl.semaphore_wait(barrier, n_fsdp + n_dp - 2)

    for kind in (0, 1):
        for way in (0, 1):
            if has(way, 1, kind):
                ring_copy(way, 1, kind, me).start()

    def multiply(q):
        first = pl.multiple_of(q * rows, rows)
        base[...] += jnp.dot(
            hid[:, pl.ds(first, rows)], weights[q, 0:rows, :], preferred_element_type=jnp.float32
        )
        left, right = acc_l[...], acc_r[...]
        for t in range(groups // 2):
            tile = weights[q, rows:rows + PACK, t * LANES:(t + 1) * LANES]
            begin = pl.multiple_of(q * rows + 2 * t * PACK, PACK)
            left += jnp.dot(hid[:, pl.ds(begin, PACK)], tile, preferred_element_type=jnp.float32)
            begin = pl.multiple_of(q * rows + (2 * t + 1) * PACK, PACK)
            right += jnp.dot(hid[:, pl.ds(begin, PACK)], tile, preferred_element_type=jnp.float32)
        acc_l[...] = left
        acc_r[...] = right

    base[...] = jnp.zeros_like(base)
    acc_l[...] = jnp.zeros_like(acc_l)
    acc_r[...] = jnp.zeros_like(acc_r)
    hid_copy.wait()
    multiply(me)

    def take_ring(s, kind):
        for way in (0, 1):
            if has(way, s, kind):
                q = shard_of(way, s)
                ring_copy(way, s, kind, q).wait_recv()
                if has(way, s + 1, kind):
                    ring_copy(way, s + 1, kind, q).start()
                if kind == 0:
                    x_copy(way, s, q, own[0]).start()
                core_copy(way, s, kind, q, own[kind]).start()

    def take_x(s):
        for way in (0, 1):
            if has(way, s, 0):
                q = shard_of(way, s)
                x_copy(way, s, q, x_own).wait_recv()
                core_copy(way, s, 2, q, x_own).start()

    def finish(s):
        for way in (0, 1):
            for kind in (0, 1, 2):
                if has(way, s, kind % 2):
                    core_copy(way, s, kind, shard_of(way, s), core_own[kind]).wait_recv()
        if s == half:
            multiply(shard_of(0, s))
        else:
            def both(i, _):
                multiply(at(pos + s * (2 * i - 1)))
                return 0
            lax.fori_loop(0, 2, both, 0)

    for s in range(1, half + 1):
        take_ring(s, 0)
        if s > 1:
            take_x(s - 1)
        take_ring(s, 1)
        if s > 1:
            finish(s - 1)
    take_x(half)
    finish(half)

    low = (acc_l[:, 0:rank] + acc_r[:, rank:2 * rank]).astype(jnp.bfloat16)
    ref_act = base[...]
    policy = ref_act + ADAPTER_SCALE * jnp.dot(low, up_ref[...], preferred_element_type=jnp.float32)
    t_policy = jnp.tanh(policy)
    read_copy.wait()
    resp = resp_ref[...].astype(jnp.float32)
    masks = [
        jnp.transpose(jnp.broadcast_to(resp[i:i + 1, :], (seq, seq)))[:, 0:1] for i in (0, 1)
    ]
    mask = jnp.concatenate(masks, axis=0)
    weighted = read[...].astype(jnp.float32) * mask
    scores = weighted * (t_policy - jnp.tanh(ref_act))
    diff = scores[0:seq, :] - scores[seq:, :]
    tile = jnp.zeros((seq, LANES), jnp.float32)
    for t in range(diff.shape[1] // LANES):
        tile += diff[:, t * LANES:(t + 1) * LANES]
    ratio_buf[me] = jnp.sum(tile.reshape(seq // 8, 8, LANES), axis=0)

    def ratio_copy(k):
        return remote(
            ratio_buf.at[me], ratio_buf.at[me], ratio_s.at[k], ratio_r.at[k], fsdp=lax.rem(me + k, n_fsdp)
        )

    def each(first, last, body):
        def step(k, _):
            body(k)
            return 0
        lax.fori_loop(first, last, step, 0)

    each(1, n_fsdp, lambda k: ratio_copy(k).start())
    slope = DPO_BETA * weighted * (1.0 - t_policy * t_policy)
    grad_h = jnp.concatenate([-slope[0:seq, :], slope[seq:, :]], axis=0).astype(jnp.bfloat16)
    grad_low = ADAPTER_SCALE * lax.dot_general(
        grad_h, up_ref[...], (((1,), (1,)), ((), ())), preferred_element_type=jnp.float32
    )
    grad_low_t[...] = jnp.transpose(grad_low).astype(jnp.bfloat16)
    grad_b_t = ADAPTER_SCALE * lax.dot_general(
        grad_h, low, (((0,), (0,)), ((), ())), preferred_element_type=jnp.float32
    )
    for q in range(n_fsdp):
        block = grad_b_t[q * up_rows:(q + 1) * up_rows, :]
        block = jnp.concatenate([block, jnp.zeros((up_rows, LANES - rank), jnp.float32)], axis=1)
        if up_rows < rank:
            block = jnp.concatenate([block, jnp.zeros((rank - up_rows, LANES), jnp.float32)], axis=0)
        part[q, :, rows:rows + LANES] = block

    half_rows, quarter = rank // 2, rank // 4
    mine1 = pl.multiple_of(core * half_rows, half_rows)
    theirs1 = pl.multiple_of((1 - core) * half_rows, half_rows)

    def block_of(k):
        return lax.rem(me + k, n_fsdp)

    def copy1(k):
        return remote(
            part.at[block_of(k), pl.ds(theirs1, half_rows), :], buf1.at[k], s1.at[k], r1.at[k], dp=core_peer
        )

    def copy2(k):
        return remote(send2.at[k], buf2.at[k], s2.at[k], r2.at[k], dp=x_peer)

    def copy3(k):
        return remote(send3.at[k], buf3.at[k], s3.at[k], r3.at[k], fsdp=block_of(k))

    def stage1(k):
        q = block_of(k)
        part[q, :, 0:rows] = jnp.dot(
            grad_low_t[...], hid[:, pl.ds(pl.multiple_of(q * rows, rows), rows)],
            preferred_element_type=jnp.float32,
        )

    def stage2(k):
        q = block_of(k)
        copy1(k).wait_recv()
        give = pl.multiple_of((1 - xbit) * quarter, quarter)
        keep = pl.multiple_of(xbit * quarter, quarter)
        send2[k] = (part[q, pl.ds(mine1 + give, quarter), :] + buf1[k, pl.ds(give, quarter), :]).astype(jnp.bfloat16)
        copy2(k).start()
        total2[k] = part[q, pl.ds(mine1 + keep, quarter), :] + buf1[k, pl.ds(keep, quarter), :]

    def stage3(k):
        copy2(k).wait_recv()
        send3[k] = (total2[k] + buf2[k].astype(jnp.float32)).astype(jnp.bfloat16)
        copy3(k).start()

    each(0, n_fsdp, stage1)

    each(1, n_fsdp, lambda k: ratio_copy(k).wait())
    margin = DPO_BETA * jnp.sum(jnp.sum(ratio_buf[...], axis=0), keepdims=True)
    loss = jnp.maximum(-margin, 0.0) + jnp.log1p(jnp.exp(-jnp.abs(margin)))
    gate = 1.0 / (1.0 + jnp.exp(margin))

    def send1(k):
        q = block_of(k)
        part[q] = part[q] * gate
        copy1(k).start()

    each(1, n_fsdp, send1)
    send1(0)
    each(1, n_fsdp, stage2)
    stage2(0)
    each(1, n_fsdp, stage3)
    copy2(0).wait_recv()
    total2[0] = total2[0] + buf2[0].astype(jnp.float32)

    def stage4(k):
        copy3(k).wait_recv()
        total2[0] = total2[0] + buf3[k].astype(jnp.float32)

    each(1, n_fsdp, stage4)
    final[0] = total2[0]

    def copy4(k):
        return remote(final.at[0], final.at[k], s4.at[k], r4.at[k], dp=lax.rem(d + k, n_dp))

    each(1, n_dp, lambda k: copy4(k).start())

    for s in range(1, half + 1):
        for way in (0, 1):
            for kind in (0, 1):
                if has(way, s, kind):
                    ring_copy(way, s, kind, me).wait_send()
                    core_copy(way, s, kind, me, own[kind]).wait_send()
            if has(way, s, 0):
                x_copy(way, s, me, own[0]).wait_send()
                core_copy(way, s, 2, me, x_own).wait_send()
    each(0, n_fsdp, lambda k: copy1(k).wait_send())
    each(0, n_fsdp, lambda k: copy2(k).wait_send())
    each(1, n_fsdp, lambda k: copy3(k).wait_send())

    each(1, n_dp, lambda k: copy4(k).wait())
    for c in (0, 1):
        for x in (0, 1):
            begin = c * half_rows + x * quarter
            total = jnp.zeros((quarter, rows + LANES), jnp.float32)
            for h in range(n_dp // 4):
                slot = lax.rem(d - (h * 4 + x * 2 + c) + n_dp, n_dp)
                total += final[slot]
            out[begin:begin + quarter, :] = total
    wide = rows + LANES
    out[rank:rank + 8, :] = jnp.broadcast_to(loss, (8, wide))
    out[rank + 8:rank + 16, :] = jnp.broadcast_to(margin, (8, wide))


def unpack(joined, down_out, up_out, loss_out, margin_out):
    rank, rows = down_out.shape
    up_rows = up_out.shape[0]
    down_out[...] = joined[0:rank, 0:rows]
    up_out[...] = joined[0:up_rows, rows:rows + up_out.shape[1]]
    loss_out[0] = jnp.max(joined[rank:rank + 8, 0:LANES])
    margin_out[0] = jnp.max(joined[rank + 8:rank + 16, 0:LANES])


def shards(n_dp, n_fsdp, hidden_input, readout, response, value_matrix, adapter_down, adapter_up):
    seq = hidden_input.shape[2]
    tokens = 2 * seq
    model = hidden_input.shape[3]
    rows, features = value_matrix.shape
    rank = adapter_down.shape[1]
    half = n_fsdp // 2
    quarter = rank // 4
    wide = rows + LANES
    f32, bf16 = jnp.float32, jnp.bfloat16
    vmem = pl.BlockSpec(memory_space=pltpu.VMEM)
    hbm = pl.BlockSpec(memory_space=pl.ANY)
    dma = pltpu.SemaphoreType.DMA
    joined = pl.pallas_call(
        functools.partial(kernel, n_dp, n_fsdp),
        out_shape=jax.ShapeDtypeStruct((rank + 16, wide), f32),
        in_specs=[hbm, hbm, vmem, hbm, vmem, vmem],
        out_specs=vmem,
        scratch_shapes=[
            pltpu.VMEM((tokens, model), bf16),
            pltpu.VMEM((tokens, features), bf16),
            pltpu.VMEM((n_fsdp, rows + PACK, features), bf16),
            pltpu.VMEM((tokens, features), f32),
            pltpu.VMEM((tokens, LANES), f32),
            pltpu.VMEM((tokens, LANES), f32),
            pltpu.VMEM((rank, tokens), bf16),
            pltpu.VMEM((n_fsdp, 8, LANES), f32),
            pltpu.VMEM((n_fsdp, rank, wide), f32),
            pltpu.VMEM((n_fsdp, rank // 2, wide), f32),
            pltpu.VMEM((n_fsdp, quarter, wide), bf16),
            pltpu.VMEM((n_fsdp, quarter, wide), bf16),
            pltpu.VMEM((n_fsdp, quarter, wide), f32),
            pltpu.VMEM((n_fsdp, quarter, wide), bf16),
            pltpu.VMEM((n_fsdp, quarter, wide), bf16),
            pltpu.VMEM((n_dp, quarter, wide), f32),
            dma((3,)),
            dma((2, half, 2)), dma((2, half, 2)),
            dma((2, half)), dma((2, half)),
            dma((2, half, 3)), dma((2, half, 3)),
            dma((n_fsdp,)), dma((n_fsdp,)),
            dma((n_fsdp,)), dma((n_fsdp,)),
            dma((n_fsdp,)), dma((n_fsdp,)),
            dma((n_fsdp,)), dma((n_fsdp,)),
            dma((n_dp,)), dma((n_dp,)),
        ],
        compiler_params=pltpu.CompilerParams(
            collective_id=0, has_side_effects=True, vmem_limit_bytes=56 << 20
        ),
        name="dpo_adapter_gradient",
    )(
        hidden_input.reshape(tokens, model),
        readout.reshape(tokens, features),
        response.reshape(2, seq),
        value_matrix,
        adapter_down.T,
        adapter_up,
    )
    smem = pl.BlockSpec(memory_space=pltpu.SMEM)
    down_t, up_block, loss, margin = pl.pallas_call(
        unpack,
        out_shape=(
            jax.ShapeDtypeStruct((rank, rows), f32),
            jax.ShapeDtypeStruct((features // n_fsdp, rank), f32),
            jax.ShapeDtypeStruct((1,), f32),
            jax.ShapeDtypeStruct((1,), f32),
        ),
        in_specs=[vmem],
        out_specs=(vmem, vmem, smem, smem),
        name="unpack_gradients",
    )(joined)
    return down_t.T, up_block, loss, margin


def solution(mesh):
    placed = (
        P("dp", None, "fsdp", None),
        P("dp", None, "fsdp", None),
        P("dp", None, "fsdp"),
        P("fsdp", None),
        P("fsdp", None),
        P(),
    )
    return jax.shard_map(
        functools.partial(shards, mesh.shape["dp"], mesh.shape["fsdp"]),
        mesh=mesh,
        in_specs=placed,
        out_specs=(P("fsdp", None), P("fsdp", None), P("dp"), P("dp")),
        check_vma=False,
    )
```

```python
import functools

import jax
import jax.numpy as jnp
from jax import lax
from jax.experimental import pallas as pl
from jax.experimental.pallas import tpu as pltpu
from jax.sharding import PartitionSpec as P

DPO_BETA = 0.5
ADAPTER_SCALE = 2.0
LANES = 128
PACK = 128
MESH = pl.DeviceIdType.MESH


def kernel(
    n_dp, n_fsdp,
    hid_hbm, read_hbm, resp_ref, value_hbm, down_ref, up_ref,
    out,
    hid, read, weighted, weights, base, acc_l, acc_r, grad_low_t,
    ratio_buf, part, buf1, send2, buf2, total2, send3, buf3, final,
    local_sem, ring_s, ring_r, x_s, x_r, core_s, core_r,
    ratio_s, ratio_r, s1, r1, s2, r2, s3, r3, s4, r4,
):
    half = n_fsdp // 2
    rows = value_hbm.shape[0]
    rank = down_ref.shape[0]
    tokens = hid.shape[0]
    seq = tokens // 2
    swapped = weights.shape[1] * 11 // 72 // 16 * 16
    kept = (weights.shape[1] - 4 * swapped) // 2
    groups = rows // PACK
    up_rows = base.shape[1] // n_fsdp

    me = lax.axis_index("fsdp")
    d = lax.axis_index("dp")
    core = lax.rem(d, 2)
    xbit = lax.rem(lax.div(d, 2), 2)
    core_peer = d + 1 - 2 * core
    x_peer = d + 2 - 4 * xbit

    col, row = lax.rem(me, 2), lax.div(me, 2)
    pos = row * (1 - col) + (n_fsdp - 1 - row) * col

    def at(p):
        p = lax.rem(p + 2 * n_fsdp, n_fsdp)
        c = lax.div(p, half)
        r = p * (1 - c) + (n_fsdp - 1 - p) * c
        return 2 * r + c

    ring_peer = (at(pos + 1), at(pos - 1))

    def shard_of(way, s):
        return at(pos - s) if way == 0 else at(pos + s)

    def piece(q, kind, p):
        if kind == 1:
            return weights.at[q, pl.ds(pl.multiple_of(4 * swapped + p * kept, 16), kept), :]
        return weights.at[q, pl.ds(pl.multiple_of(p * swapped, 16), swapped), :]

    own = (xbit * 2 + core, core)
    x_own = (1 - xbit) * 2 + core
    core_own = (xbit * 2 + 1 - core, 1 - core, (1 - xbit) * 2 + 1 - core)

    def remote(src, dst, send, recv, **where):
        return pltpu.make_async_remote_copy(
            src_ref=src, dst_ref=dst, send_sem=send, recv_sem=recv,
            device_id=where, device_id_type=MESH,
        )

    def ring_copy(way, s, kind, q):
        ref = piece(q, kind, own[kind])
        return remote(ref, ref, ring_s.at[way, s - 1, kind], ring_r.at[way, s - 1, kind], fsdp=ring_peer[way])

    def x_copy(way, s, q, p):
        ref = piece(q, 0, p)
        return remote(ref, ref, x_s.at[way, s - 1], x_r.at[way, s - 1], dp=x_peer)

    def core_copy(way, s, kind, q, p):
        ref = piece(q, kind, p)
        return remote(ref, ref, core_s.at[way, s - 1, kind], core_r.at[way, s - 1, kind], dp=core_peer)

    def has(way, s, kind):
        return s < half or (s == half and way == kind)

    value_copy = pltpu.make_async_copy(value_hbm, weights.at[me, pl.ds(0, rows), :], local_sem.at[0])
    hid_copy = pltpu.make_async_copy(hid_hbm, hid, local_sem.at[1])
    read_copy = pltpu.make_async_copy(read_hbm, read, local_sem.at[2])
    value_copy.start()
    hid_copy.start()
    read_copy.start()

    barrier = pltpu.get_barrier_semaphore()

    def greet_fsdp(k, _):
        pl.semaphore_signal(barrier, inc=1, device_id={"fsdp": lax.rem(me + k, n_fsdp)}, device_id_type=MESH)
        return 0

    def greet_dp(k, _):
        pl.semaphore_signal(barrier, inc=1, device_id={"dp": lax.rem(d + k, n_dp)}, device_id_type=MESH)
        return 0

    lax.fori_loop(1, n_fsdp, greet_fsdp, 0)
    lax.fori_loop(1, n_dp, greet_dp, 0)

    for t in range(groups // 2):
        pair = [down_ref[:, g * PACK:(g + 1) * PACK].astype(jnp.float32) for g in (2 * t, 2 * t + 1)]
        tile = jnp.transpose(jnp.concatenate(pair, axis=0)).astype(jnp.bfloat16)
        weights[me, rows:rows + PACK, t * LANES:(t + 1) * LANES] = tile
    used = groups // 2 * LANES
    if used < weights.shape[2]:
        weights[me, rows:rows + PACK, used:] = jnp.zeros((PACK, weights.shape[2] - used), jnp.bfloat16)

    value_copy.wait()
    pl.semaphore_wait(barrier, n_fsdp + n_dp - 2)

    for kind in (0, 1):
        for way in (0, 1):
            if has(way, 1, kind):
                ring_copy(way, 1, kind, me).start()

    early = 4 * swapped // PACK * PACK

    def multiply_early(q):
        first = pl.multiple_of(q * rows, PACK)
        base[...] += jnp.dot(
            hid[:, pl.ds(first, early)], weights[q, 0:early, :], preferred_element_type=jnp.float32
        )

    def multiply_late(q):
        if early < rows:
            first = pl.multiple_of(q * rows + early, PACK)
            base[...] += jnp.dot(
                hid[:, pl.ds(first, rows - early)], weights[q, early:rows, :], preferred_element_type=jnp.float32
            )
        left, right = acc_l[...], acc_r[...]
        for t in range(groups // 2):
            tile = weights[q, rows:rows + PACK, t * LANES:(t + 1) * LANES]
            begin = pl.multiple_of(q * rows + 2 * t * PACK, PACK)
            left += jnp.dot(hid[:, pl.ds(begin, PACK)], tile, preferred_element_type=jnp.float32)
            begin = pl.multiple_of(q * rows + (2 * t + 1) * PACK, PACK)
            right += jnp.dot(hid[:, pl.ds(begin, PACK)], tile, preferred_element_type=jnp.float32)
        acc_l[...] = left
        acc_r[...] = right

    base[...] = jnp.zeros_like(base)
    acc_l[...] = jnp.zeros_like(acc_l)
    acc_r[...] = jnp.zeros_like(acc_r)
    hid_copy.wait()
    multiply_early(me)
    multiply_late(me)

    read_copy.wait()
    resp = resp_ref[...].astype(jnp.float32)
    masks = [
        jnp.transpose(jnp.broadcast_to(resp[i:i + 1, :], (seq, seq)))[:, 0:1] for i in (0, 1)
    ]
    weighted[...] = read[...].astype(jnp.float32) * jnp.concatenate(masks, axis=0)

    def overtaken(way, s, kind):
        return half >= 3 and way == 0 and s == half - 1 and kind == 1

    def take_ring(way, s, kind):
        if not has(way, s, kind):
            return
        q = shard_of(way, s)
        ring_copy(way, s, kind, q).wait_recv()
        if has(way, s + 1, kind) and not overtaken(way, s + 1, kind):
            ring_copy(way, s + 1, kind, q).start()
        if kind == 0 and overtaken(way, s, 1):
            ring_copy(way, s, 1, shard_of(way, s - 1)).start()
        if kind == 0:
            x_copy(way, s, q, own[0]).start()
        core_copy(way, s, kind, q, own[kind]).start()

    def take_x(way, s):
        if has(way, s, 0):
            q = shard_of(way, s)
            x_copy(way, s, q, x_own).wait_recv()
            core_copy(way, s, 2, q, x_own).start()

    def take_core(way, s, kind):
        if has(way, s, kind % 2):
            core_copy(way, s, kind, shard_of(way, s), core_own[kind]).wait_recv()

    def finish_early(s):
        for way in (0, 1):
            take_core(way, s, 0)
            take_core(way, s, 2)
        for way in ((0, 1) if s < half else (0,)):
            multiply_early(shard_of(way, s))

    def finish_late(way, s):
        take_core(way, s, 1)
        multiply_late(shard_of(way, s))

    for s in range(1, half):
        for way in (0, 1):
            take_ring(way, s, 0)
        if s > 1:
            for way in (0, 1):
                take_x(way, s - 1)
            finish_early(s - 1)
            for way in (0, 1):
                finish_late(way, s - 1)
        if s < half - 1:
            for way in (0, 1):
                take_ring(way, s, 1)
    take_ring(0, half, 0)
    take_ring(1, half - 1, 1)
    for way in (0, 1):
        take_x(way, half - 1)
    finish_early(half - 1)
    finish_late(1, half - 1)
    take_ring(0, half - 1, 1)
    take_ring(1, half, 1)
    take_x(0, half)
    finish_late(0, half - 1)
    finish_early(half)
    finish_late(1, half)

    low = (acc_l[:, 0:rank] + acc_r[:, rank:2 * rank]).astype(jnp.bfloat16)
    ref_act = base[...]
    policy = ref_act + ADAPTER_SCALE * jnp.dot(low, up_ref[...], preferred_element_type=jnp.float32)
    t_policy = jnp.tanh(policy)
    scores = weighted[...] * (t_policy - jnp.tanh(ref_act))
    diff = scores[0:seq, :] - scores[seq:, :]
    tile = jnp.zeros((seq, LANES), jnp.float32)
    for t in range(diff.shape[1] // LANES):
        tile += diff[:, t * LANES:(t + 1) * LANES]
    ratio_buf[me] = jnp.sum(tile.reshape(seq // 8, 8, LANES), axis=0)

    def ratio_copy(k):
        return remote(
            ratio_buf.at[me], ratio_buf.at[me], ratio_s.at[k], ratio_r.at[k], fsdp=lax.rem(me + k, n_fsdp)
        )

    def each(first, last, body):
        def step(k, _):
            body(k)
            return 0
        lax.fori_loop(first, last, step, 0)

    each(1, n_fsdp, lambda k: ratio_copy(k).start())
    slope = DPO_BETA * weighted[...] * (1.0 - t_policy * t_policy)
    grad_h = jnp.concatenate([-slope[0:seq, :], slope[seq:, :]], axis=0).astype(jnp.bfloat16)
    grad_low = ADAPTER_SCALE * lax.dot_general(
        grad_h, up_ref[...], (((1,), (1,)), ((), ())), preferred_element_type=jnp.float32
    )
    grad_low_t[...] = jnp.transpose(grad_low).astype(jnp.bfloat16)
    grad_b_t = ADAPTER_SCALE * lax.dot_general(
        grad_h, low, (((0,), (0,)), ((), ())), preferred_element_type=jnp.float32
    )
    for q in range(n_fsdp):
        block = grad_b_t[q * up_rows:(q + 1) * up_rows, :]
        block = jnp.concatenate([block, jnp.zeros((up_rows, LANES - rank), jnp.float32)], axis=1)
        if up_rows < rank:
            block = jnp.concatenate([block, jnp.zeros((rank - up_rows, LANES), jnp.float32)], axis=0)
        part[q, :, rows:rows + LANES] = block

    half_rows, quarter = rank // 2, rank // 4
    mine1 = pl.multiple_of(core * half_rows, half_rows)
    theirs1 = pl.multiple_of((1 - core) * half_rows, half_rows)

    def block_of(k):
        return lax.rem(me + k, n_fsdp)

    def copy1(k):
        return remote(
            part.at[block_of(k), pl.ds(theirs1, half_rows), :], buf1.at[k], s1.at[k], r1.at[k], dp=core_peer
        )

    def copy2(k):
        return remote(send2.at[k], buf2.at[k], s2.at[k], r2.at[k], dp=x_peer)

    def copy3(k):
        return remote(send3.at[k], buf3.at[k], s3.at[k], r3.at[k], fsdp=block_of(k))

    def stage1(k):
        q = block_of(k)
        part[q, :, 0:rows] = jnp.dot(
            grad_low_t[...], hid[:, pl.ds(pl.multiple_of(q * rows, rows), rows)],
            preferred_element_type=jnp.float32,
        )

    def stage2(k):
        q = block_of(k)
        copy1(k).wait_recv()
        give = pl.multiple_of((1 - xbit) * quarter, quarter)
        keep = pl.multiple_of(xbit * quarter, quarter)
        send2[k] = (part[q, pl.ds(mine1 + give, quarter), :] + buf1[k, pl.ds(give, quarter), :]).astype(jnp.bfloat16)
        copy2(k).start()
        total2[k] = part[q, pl.ds(mine1 + keep, quarter), :] + buf1[k, pl.ds(keep, quarter), :]

    def stage3(k):
        copy2(k).wait_recv()
        send3[k] = (total2[k] + buf2[k].astype(jnp.float32)).astype(jnp.bfloat16)
        copy3(k).start()

    each(0, n_fsdp, stage1)

    each(1, n_fsdp, lambda k: ratio_copy(k).wait())
    margin = DPO_BETA * jnp.sum(jnp.sum(ratio_buf[...], axis=0), keepdims=True)
    loss = jnp.maximum(-margin, 0.0) + jnp.log1p(jnp.exp(-jnp.abs(margin)))
    gate = 1.0 / (1.0 + jnp.exp(margin))

    def send1(k):
        q = block_of(k)
        part[q] = part[q] * gate
        copy1(k).start()

    each(1, n_fsdp, send1)
    send1(0)
    each(1, n_fsdp, stage2)
    stage2(0)
    each(1, n_fsdp, stage3)
    copy2(0).wait_recv()
    total2[0] = total2[0] + buf2[0].astype(jnp.float32)

    def stage4(k):
        copy3(k).wait_recv()
        total2[0] = total2[0] + buf3[k].astype(jnp.float32)

    each(1, n_fsdp, stage4)
    final[0] = total2[0]

    def copy4(k):
        return remote(final.at[0], final.at[k], s4.at[k], r4.at[k], dp=lax.rem(d + k, n_dp))

    each(1, n_dp, lambda k: copy4(k).start())

    for s in range(1, half + 1):
        for way in (0, 1):
            for kind in (0, 1):
                if has(way, s, kind):
                    ring_copy(way, s, kind, me).wait_send()
                    core_copy(way, s, kind, me, own[kind]).wait_send()
            if has(way, s, 0):
                x_copy(way, s, me, own[0]).wait_send()
                core_copy(way, s, 2, me, x_own).wait_send()
    each(0, n_fsdp, lambda k: copy1(k).wait_send())
    each(0, n_fsdp, lambda k: copy2(k).wait_send())
    each(1, n_fsdp, lambda k: copy3(k).wait_send())

    each(1, n_dp, lambda k: copy4(k).wait())
    for c in (0, 1):
        for x in (0, 1):
            begin = c * half_rows + x * quarter
            total = jnp.zeros((quarter, rows + LANES), jnp.float32)
            for h in range(n_dp // 4):
                slot = lax.rem(d - (h * 4 + x * 2 + c) + n_dp, n_dp)
                total += final[slot]
            out[begin:begin + quarter, :] = total
    wide = rows + LANES
    out[rank:rank + 8, :] = jnp.broadcast_to(loss, (8, wide))
    out[rank + 8:rank + 16, :] = jnp.broadcast_to(margin, (8, wide))


def unpack(joined, down_out, up_out, loss_out, margin_out):
    rank, rows = down_out.shape
    up_rows = up_out.shape[0]
    down_out[...] = joined[0:rank, 0:rows]
    up_out[...] = joined[0:up_rows, rows:rows + up_out.shape[1]]
    loss_out[0] = jnp.max(joined[rank:rank + 8, 0:LANES])
    margin_out[0] = jnp.max(joined[rank + 8:rank + 16, 0:LANES])


def shards(n_dp, n_fsdp, hidden_input, readout, response, value_matrix, adapter_down, adapter_up):
    seq = hidden_input.shape[2]
    tokens = 2 * seq
    model = hidden_input.shape[3]
    rows, features = value_matrix.shape
    rank = adapter_down.shape[1]
    half = n_fsdp // 2
    quarter = rank // 4
    wide = rows + LANES
    f32, bf16 = jnp.float32, jnp.bfloat16
    vmem = pl.BlockSpec(memory_space=pltpu.VMEM)
    hbm = pl.BlockSpec(memory_space=pl.ANY)
    dma = pltpu.SemaphoreType.DMA
    joined = pl.pallas_call(
        functools.partial(kernel, n_dp, n_fsdp),
        out_shape=jax.ShapeDtypeStruct((rank + 16, wide), f32),
        in_specs=[hbm, hbm, vmem, hbm, vmem, vmem],
        out_specs=vmem,
        scratch_shapes=[
            pltpu.VMEM((tokens, model), bf16),
            pltpu.VMEM((tokens, features), bf16),
            pltpu.VMEM((tokens, features), f32),
            pltpu.VMEM((n_fsdp, rows + PACK, features), bf16),
            pltpu.VMEM((tokens, features), f32),
            pltpu.VMEM((tokens, LANES), f32),
            pltpu.VMEM((tokens, LANES), f32),
            pltpu.VMEM((rank, tokens), bf16),
            pltpu.VMEM((n_fsdp, 8, LANES), f32),
            pltpu.VMEM((n_fsdp, rank, wide), f32),
            pltpu.VMEM((n_fsdp, rank // 2, wide), f32),
            pltpu.VMEM((n_fsdp, quarter, wide), bf16),
            pltpu.VMEM((n_fsdp, quarter, wide), bf16),
            pltpu.VMEM((n_fsdp, quarter, wide), f32),
            pltpu.VMEM((n_fsdp, quarter, wide), bf16),
            pltpu.VMEM((n_fsdp, quarter, wide), bf16),
            pltpu.VMEM((n_dp, quarter, wide), f32),
            dma((3,)),
            dma((2, half, 2)), dma((2, half, 2)),
            dma((2, half)), dma((2, half)),
            dma((2, half, 3)), dma((2, half, 3)),
            dma((n_fsdp,)), dma((n_fsdp,)),
            dma((n_fsdp,)), dma((n_fsdp,)),
            dma((n_fsdp,)), dma((n_fsdp,)),
            dma((n_fsdp,)), dma((n_fsdp,)),
            dma((n_dp,)), dma((n_dp,)),
        ],
        compiler_params=pltpu.CompilerParams(
            collective_id=0, has_side_effects=True, vmem_limit_bytes=56 << 20
        ),
        name="dpo_adapter_gradient",
    )(
        hidden_input.reshape(tokens, model),
        readout.reshape(tokens, features),
        response.reshape(2, seq),
        value_matrix,
        adapter_down.T,
        adapter_up,
    )
    smem = pl.BlockSpec(memory_space=pltpu.SMEM)
    down_t, up_block, loss, margin = pl.pallas_call(
        unpack,
        out_shape=(
            jax.ShapeDtypeStruct((rank, rows), f32),
            jax.ShapeDtypeStruct((features // n_fsdp, rank), f32),
            jax.ShapeDtypeStruct((1,), f32),
            jax.ShapeDtypeStruct((1,), f32),
        ),
        in_specs=[vmem],
        out_specs=(vmem, vmem, smem, smem),
        name="unpack_gradients",
    )(joined)
    return down_t.T, up_block, loss, margin


def solution(mesh):
    placed = (
        P("dp", None, "fsdp", None),
        P("dp", None, "fsdp", None),
        P("dp", None, "fsdp"),
        P("fsdp", None),
        P("fsdp", None),
        P(),
    )
    return jax.shard_map(
        functools.partial(shards, mesh.shape["dp"], mesh.shape["fsdp"]),
        mesh=mesh,
        in_specs=placed,
        out_specs=(P("fsdp", None), P("fsdp", None), P("dp"), P("dp")),
        check_vma=False,
    )
```

```python
import functools

import jax
import jax.numpy as jnp
from jax import lax
from jax.experimental import pallas as pl
from jax.experimental.pallas import tpu as pltpu
from jax.sharding import PartitionSpec as P

DPO_BETA = 0.5
ADAPTER_SCALE = 2.0
LANES = 128
PACK = 128
MESH = pl.DeviceIdType.MESH


def kernel(
    n_dp, n_fsdp,
    hid_hbm, read_hbm, resp_ref, value_hbm, down_ref, up_ref,
    out,
    hid, read, weights, base, acc_l, acc_r, grad_low_t,
    ratio_buf, part, buf1, send2, buf2, total2, send3, buf3, final,
    local_sem, ring_s, ring_r, x_s, x_r, core_s, core_r,
    ratio_s, ratio_r, s1, r1, s2, r2, s3, r3, s4, r4,
):
    half = n_fsdp // 2
    rows = value_hbm.shape[0]
    rank = down_ref.shape[0]
    tokens = hid.shape[0]
    seq = tokens // 2
    swapped = weights.shape[1] * 13 // 72 // 16 * 16
    kept = (weights.shape[1] - 4 * swapped) // 2
    groups = rows // PACK
    up_rows = base.shape[1] // n_fsdp

    me = lax.axis_index("fsdp")
    d = lax.axis_index("dp")
    core = lax.rem(d, 2)
    xbit = lax.rem(lax.div(d, 2), 2)
    core_peer = d + 1 - 2 * core
    x_peer = d + 2 - 4 * xbit

    col, row = lax.rem(me, 2), lax.div(me, 2)
    pos = row * (1 - col) + (n_fsdp - 1 - row) * col

    def at(p):
        p = lax.rem(p + 2 * n_fsdp, n_fsdp)
        c = lax.div(p, half)
        r = p * (1 - c) + (n_fsdp - 1 - p) * c
        return 2 * r + c

    ring_peer = (at(pos + 1), at(pos - 1))

    def shard_of(way, s):
        return at(pos - s) if way == 0 else at(pos + s)

    def piece(q, kind, p):
        if kind == 1:
            return weights.at[q, pl.ds(pl.multiple_of(4 * swapped + p * kept, 16), kept), :]
        return weights.at[q, pl.ds(pl.multiple_of(p * swapped, 16), swapped), :]

    own = (xbit * 2 + core, core)
    x_own = (1 - xbit) * 2 + core
    core_own = (xbit * 2 + 1 - core, 1 - core, (1 - xbit) * 2 + 1 - core)

    def remote(src, dst, send, recv, **where):
        return pltpu.make_async_remote_copy(
            src_ref=src, dst_ref=dst, send_sem=send, recv_sem=recv,
            device_id=where, device_id_type=MESH,
        )

    def ring_copy(way, s, kind, q):
        ref = piece(q, kind, own[kind])
        return remote(ref, ref, ring_s.at[way, s - 1, kind], ring_r.at[way, s - 1, kind], fsdp=ring_peer[way])

    def x_copy(way, s, q, p):
        ref = piece(q, 0, p)
        return remote(ref, ref, x_s.at[way, s - 1], x_r.at[way, s - 1], dp=x_peer)

    def core_copy(way, s, kind, q, p):
        ref = piece(q, kind, p)
        return remote(ref, ref, core_s.at[way, s - 1, kind], core_r.at[way, s - 1, kind], dp=core_peer)

    def has(way, s, kind):
        return s < half or (s == half and way == kind)

    value_copy = pltpu.make_async_copy(value_hbm, weights.at[me, pl.ds(0, rows), :], local_sem.at[0])
    hid_copy = pltpu.make_async_copy(hid_hbm, hid, local_sem.at[1])
    read_copy = pltpu.make_async_copy(read_hbm, read, local_sem.at[2])
    value_copy.start()
    hid_copy.start()
    read_copy.start()

    barrier = pltpu.get_barrier_semaphore()

    def greet_fsdp(k, _):
        pl.semaphore_signal(barrier, inc=1, device_id={"fsdp": lax.rem(me + k, n_fsdp)}, device_id_type=MESH)
        return 0

    def greet_dp(k, _):
        pl.semaphore_signal(barrier, inc=1, device_id={"dp": lax.rem(d + k, n_dp)}, device_id_type=MESH)
        return 0

    lax.fori_loop(1, n_fsdp, greet_fsdp, 0)
    lax.fori_loop(1, n_dp, greet_dp, 0)

    for t in range(groups // 2):
        pair = [down_ref[:, g * PACK:(g + 1) * PACK].astype(jnp.float32) for g in (2 * t, 2 * t + 1)]
        tile = jnp.transpose(jnp.concatenate(pair, axis=0)).astype(jnp.bfloat16)
        weights[me, rows:rows + PACK, t * LANES:(t + 1) * LANES] = tile
    used = groups // 2 * LANES
    if used < weights.shape[2]:
        weights[me, rows:rows + PACK, used:] = jnp.zeros((PACK, weights.shape[2] - used), jnp.bfloat16)

    value_copy.wait()
    pl.semaphore_wait(barrier, n_fsdp + n_dp - 2)

    for kind in (0, 1):
        for way in (0, 1):
            if has(way, 1, kind):
                ring_copy(way, 1, kind, me).start()

    def multiply(q):
        first = pl.multiple_of(q * rows, rows)
        base[...] += jnp.dot(
            hid[:, pl.ds(first, rows)], weights[q, 0:rows, :], preferred_element_type=jnp.float32
        )
        left, right = acc_l[...], acc_r[...]
        for t in range(groups // 2):
            tile = weights[q, rows:rows + PACK, t * LANES:(t + 1) * LANES]
            begin = pl.multiple_of(q * rows + 2 * t * PACK, PACK)
            left += jnp.dot(hid[:, pl.ds(begin, PACK)], tile, preferred_element_type=jnp.float32)
            begin = pl.multiple_of(q * rows + (2 * t + 1) * PACK, PACK)
            right += jnp.dot(hid[:, pl.ds(begin, PACK)], tile, preferred_element_type=jnp.float32)
        acc_l[...] = left
        acc_r[...] = right

    base[...] = jnp.zeros_like(base)
    acc_l[...] = jnp.zeros_like(acc_l)
    acc_r[...] = jnp.zeros_like(acc_r)
    hid_copy.wait()
    multiply(me)

    def take_ring(s, kind):
        for way in (0, 1):
            if has(way, s, kind):
                q = shard_of(way, s)
                ring_copy(way, s, kind, q).wait_recv()
                if has(way, s + 1, kind):
                    ring_copy(way, s + 1, kind, q).start()
                if kind == 0:
                    x_copy(way, s, q, own[0]).start()
                core_copy(way, s, kind, q, own[kind]).start()

    def take_x(s):
        for way in (0, 1):
            if has(way, s, 0):
                q = shard_of(way, s)
                x_copy(way, s, q, x_own).wait_recv()
                core_copy(way, s, 2, q, x_own).start()

    def finish(s):
        for way in (0, 1):
            for kind in (0, 1, 2):
                if has(way, s, kind % 2):
                    core_copy(way, s, kind, shard_of(way, s), core_own[kind]).wait_recv()
        if s == half:
            multiply(shard_of(0, s))
        else:
            def both(i, _):
                multiply(at(pos + s * (2 * i - 1)))
                return 0
            lax.fori_loop(0, 2, both, 0)

    for s in range(1, half + 1):
        take_ring(s, 0)
        if s > 1:
            take_x(s - 1)
        take_ring(s, 1)
        if s > 1:
            finish(s - 1)
    take_x(half)
    finish(half)

    low = (acc_l[:, 0:rank] + acc_r[:, rank:2 * rank]).astype(jnp.bfloat16)
    ref_act = base[...]
    policy = ref_act + ADAPTER_SCALE * jnp.dot(low, up_ref[...], preferred_element_type=jnp.float32)
    t_policy = jnp.tanh(policy)
    read_copy.wait()
    resp = resp_ref[...].astype(jnp.float32)
    masks = [
        jnp.transpose(jnp.broadcast_to(resp[i:i + 1, :], (seq, seq)))[:, 0:1] for i in (0, 1)
    ]
    mask = jnp.concatenate(masks, axis=0)
    weighted = read[...].astype(jnp.float32) * mask
    scores = weighted * (t_policy - jnp.tanh(ref_act))
    diff = scores[0:seq, :] - scores[seq:, :]
    tile = jnp.zeros((seq, LANES), jnp.float32)
    for t in range(diff.shape[1] // LANES):
        tile += diff[:, t * LANES:(t + 1) * LANES]
    ratio_buf[me] = jnp.sum(tile.reshape(seq // 8, 8, LANES), axis=0)

    def ratio_copy(k):
        return remote(
            ratio_buf.at[me], ratio_buf.at[me], ratio_s.at[k], ratio_r.at[k], fsdp=lax.rem(me + k, n_fsdp)
        )

    def each(first, last, body):
        def step(k, _):
            body(k)
            return 0
        lax.fori_loop(first, last, step, 0)

    each(1, n_fsdp, lambda k: ratio_copy(k).start())
    slope = DPO_BETA * weighted * (1.0 - t_policy * t_policy)
    grad_h = jnp.concatenate([-slope[0:seq, :], slope[seq:, :]], axis=0).astype(jnp.bfloat16)
    grad_low = ADAPTER_SCALE * lax.dot_general(
        grad_h, up_ref[...], (((1,), (1,)), ((), ())), preferred_element_type=jnp.float32
    )
    grad_low_t[...] = jnp.transpose(grad_low).astype(jnp.bfloat16)
    grad_b_t = ADAPTER_SCALE * lax.dot_general(
        grad_h, low, (((0,), (0,)), ((), ())), preferred_element_type=jnp.float32
    )
    for q in range(n_fsdp):
        block = grad_b_t[q * up_rows:(q + 1) * up_rows, :]
        block = jnp.concatenate([block, jnp.zeros((up_rows, LANES - rank), jnp.float32)], axis=1)
        if up_rows < rank:
            block = jnp.concatenate([block, jnp.zeros((rank - up_rows, LANES), jnp.float32)], axis=0)
        part[q, :, rows:rows + LANES] = block

    half_rows, quarter = rank // 2, rank // 4
    mine1 = pl.multiple_of(core * half_rows, half_rows)
    theirs1 = pl.multiple_of((1 - core) * half_rows, half_rows)

    def block_of(k):
        return lax.rem(me + k, n_fsdp)

    def copy1(k):
        return remote(
            part.at[block_of(k), pl.ds(theirs1, half_rows), :], buf1.at[k], s1.at[k], r1.at[k], dp=core_peer
        )

    def copy2(k):
        return remote(send2.at[k], buf2.at[k], s2.at[k], r2.at[k], dp=x_peer)

    def copy3(k):
        return remote(send3.at[k], buf3.at[k], s3.at[k], r3.at[k], fsdp=block_of(k))

    def stage1(k):
        q = block_of(k)
        part[q, :, 0:rows] = jnp.dot(
            grad_low_t[...], hid[:, pl.ds(pl.multiple_of(q * rows, rows), rows)],
            preferred_element_type=jnp.float32,
        )

    def stage2(k):
        q = block_of(k)
        copy1(k).wait_recv()
        give = pl.multiple_of((1 - xbit) * quarter, quarter)
        keep = pl.multiple_of(xbit * quarter, quarter)
        send2[k] = (part[q, pl.ds(mine1 + give, quarter), :] + buf1[k, pl.ds(give, quarter), :]).astype(jnp.bfloat16)
        copy2(k).start()
        total2[k] = part[q, pl.ds(mine1 + keep, quarter), :] + buf1[k, pl.ds(keep, quarter), :]

    def stage3(k):
        copy2(k).wait_recv()
        send3[k] = (total2[k] + buf2[k].astype(jnp.float32)).astype(jnp.bfloat16)
        copy3(k).start()

    each(0, n_fsdp, stage1)

    each(1, n_fsdp, lambda k: ratio_copy(k).wait())
    margin = DPO_BETA * jnp.sum(jnp.sum(ratio_buf[...], axis=0), keepdims=True)
    loss = jnp.maximum(-margin, 0.0) + jnp.log1p(jnp.exp(-jnp.abs(margin)))
    gate = 1.0 / (1.0 + jnp.exp(margin))

    def send1(k):
        q = block_of(k)
        part[q] = part[q] * gate
        copy1(k).start()

    each(1, n_fsdp, send1)
    send1(0)
    each(1, n_fsdp, stage2)
    stage2(0)
    each(1, n_fsdp, stage3)
    copy2(0).wait_recv()
    total2[0] = total2[0] + buf2[0].astype(jnp.float32)

    def stage4(k):
        copy3(k).wait_recv()
        total2[0] = total2[0] + buf3[k].astype(jnp.float32)

    each(1, n_fsdp, stage4)
    final[0] = total2[0]

    def copy4(k):
        return remote(final.at[0], final.at[k], s4.at[k], r4.at[k], dp=lax.rem(d + k, n_dp))

    each(1, n_dp, lambda k: copy4(k).start())

    for s in range(1, half + 1):
        for way in (0, 1):
            for kind in (0, 1):
                if has(way, s, kind):
                    ring_copy(way, s, kind, me).wait_send()
                    core_copy(way, s, kind, me, own[kind]).wait_send()
            if has(way, s, 0):
                x_copy(way, s, me, own[0]).wait_send()
                core_copy(way, s, 2, me, x_own).wait_send()
    each(0, n_fsdp, lambda k: copy1(k).wait_send())
    each(0, n_fsdp, lambda k: copy2(k).wait_send())
    each(1, n_fsdp, lambda k: copy3(k).wait_send())

    each(1, n_dp, lambda k: copy4(k).wait())
    for c in (0, 1):
        for x in (0, 1):
            begin = c * half_rows + x * quarter
            total = jnp.zeros((quarter, rows + LANES), jnp.float32)
            for h in range(n_dp // 4):
                slot = lax.rem(d - (h * 4 + x * 2 + c) + n_dp, n_dp)
                total += final[slot]
            out[begin:begin + quarter, :] = total
    wide = rows + LANES
    out[rank:rank + 8, :] = jnp.broadcast_to(loss, (8, wide))
    out[rank + 8:rank + 16, :] = jnp.broadcast_to(margin, (8, wide))


def unpack(joined, down_out, up_out, loss_out, margin_out):
    rank, rows = down_out.shape
    up_rows = up_out.shape[0]
    down_out[...] = joined[0:rank, 0:rows]
    up_out[...] = joined[0:up_rows, rows:rows + up_out.shape[1]]
    loss_out[0] = jnp.max(joined[rank:rank + 8, 0:LANES])
    margin_out[0] = jnp.max(joined[rank + 8:rank + 16, 0:LANES])


def shards(n_dp, n_fsdp, hidden_input, readout, response, value_matrix, adapter_down, adapter_up):
    seq = hidden_input.shape[2]
    tokens = 2 * seq
    model = hidden_input.shape[3]
    rows, features = value_matrix.shape
    rank = adapter_down.shape[1]
    half = n_fsdp // 2
    quarter = rank // 4
    wide = rows + LANES
    f32, bf16 = jnp.float32, jnp.bfloat16
    vmem = pl.BlockSpec(memory_space=pltpu.VMEM)
    hbm = pl.BlockSpec(memory_space=pl.ANY)
    dma = pltpu.SemaphoreType.DMA
    joined = pl.pallas_call(
        functools.partial(kernel, n_dp, n_fsdp),
        out_shape=jax.ShapeDtypeStruct((rank + 16, wide), f32),
        in_specs=[hbm, hbm, vmem, hbm, vmem, vmem],
        out_specs=vmem,
        scratch_shapes=[
            pltpu.VMEM((tokens, model), bf16),
            pltpu.VMEM((tokens, features), bf16),
            pltpu.VMEM((n_fsdp, rows + PACK, features), bf16),
            pltpu.VMEM((tokens, features), f32),
            pltpu.VMEM((tokens, LANES), f32),
            pltpu.VMEM((tokens, LANES), f32),
            pltpu.VMEM((rank, tokens), bf16),
            pltpu.VMEM((n_fsdp, 8, LANES), f32),
            pltpu.VMEM((n_fsdp, rank, wide), f32),
            pltpu.VMEM((n_fsdp, rank // 2, wide), f32),
            pltpu.VMEM((n_fsdp, quarter, wide), bf16),
            pltpu.VMEM((n_fsdp, quarter, wide), bf16),
            pltpu.VMEM((n_fsdp, quarter, wide), f32),
            pltpu.VMEM((n_fsdp, quarter, wide), bf16),
            pltpu.VMEM((n_fsdp, quarter, wide), bf16),
            pltpu.VMEM((n_dp, quarter, wide), f32),
            dma((3,)),
            dma((2, half, 2)), dma((2, half, 2)),
            dma((2, half)), dma((2, half)),
            dma((2, half, 3)), dma((2, half, 3)),
            dma((n_fsdp,)), dma((n_fsdp,)),
            dma((n_fsdp,)), dma((n_fsdp,)),
            dma((n_fsdp,)), dma((n_fsdp,)),
            dma((n_fsdp,)), dma((n_fsdp,)),
            dma((n_dp,)), dma((n_dp,)),
        ],
        compiler_params=pltpu.CompilerParams(
            collective_id=0, has_side_effects=True, vmem_limit_bytes=56 << 20
        ),
        name="dpo_adapter_gradient",
    )(
        hidden_input.reshape(tokens, model),
        readout.reshape(tokens, features),
        response.reshape(2, seq),
        value_matrix,
        adapter_down.T,
        adapter_up,
    )
    smem = pl.BlockSpec(memory_space=pltpu.SMEM)
    down_t, up_block, loss, margin = pl.pallas_call(
        unpack,
        out_shape=(
            jax.ShapeDtypeStruct((rank, rows), f32),
            jax.ShapeDtypeStruct((features // n_fsdp, rank), f32),
            jax.ShapeDtypeStruct((1,), f32),
            jax.ShapeDtypeStruct((1,), f32),
        ),
        in_specs=[vmem],
        out_specs=(vmem, vmem, smem, smem),
        name="unpack_gradients",
    )(joined)
    return down_t.T, up_block, loss, margin


def solution(mesh):
    placed = (
        P("dp", None, "fsdp", None),
        P("dp", None, "fsdp", None),
        P("dp", None, "fsdp"),
        P("fsdp", None),
        P("fsdp", None),
        P(),
    )
    return jax.shard_map(
        functools.partial(shards, mesh.shape["dp"], mesh.shape["fsdp"]),
        mesh=mesh,
        in_specs=placed,
        out_specs=(P("fsdp", None), P("fsdp", None), P("dp"), P("dp")),
        check_vma=False,
    )
```

```python
import functools

import jax
import jax.numpy as jnp
from jax import lax
from jax.experimental import pallas as pl
from jax.experimental.pallas import tpu as pltpu
from jax.sharding import PartitionSpec as P

DPO_BETA = 0.5
ADAPTER_SCALE = 2.0
LANES = 128
PACK = 128
MESH = pl.DeviceIdType.MESH


def kernel(
    n_dp, n_fsdp,
    hid_hbm, read_hbm, resp_ref, value_hbm, down_ref, up_ref,
    out,
    hid, read, weighted, weights, base, acc_l, acc_r, grad_low_t,
    ratio_buf, part, buf1, send2, buf2, total2, send3, buf3, final,
    local_sem, ring_s, ring_r, x_s, x_r, core_s, core_r,
    ratio_s, ratio_r, s1, r1, s2, r2, s3, r3, s4, r4,
):
    half = n_fsdp // 2
    rows = value_hbm.shape[0]
    rank = down_ref.shape[0]
    tokens = hid.shape[0]
    seq = tokens // 2
    swapped = weights.shape[1] * 11 // 72 // 16 * 16
    kept = (weights.shape[1] - 4 * swapped) // 2
    groups = rows // PACK
    up_rows = base.shape[1] // n_fsdp

    me = lax.axis_index("fsdp")
    d = lax.axis_index("dp")
    core = lax.rem(d, 2)
    xbit = lax.rem(lax.div(d, 2), 2)
    core_peer = d + 1 - 2 * core
    x_peer = d + 2 - 4 * xbit

    col, row = lax.rem(me, 2), lax.div(me, 2)
    pos = row * (1 - col) + (n_fsdp - 1 - row) * col

    def at(p):
        p = lax.rem(p + 2 * n_fsdp, n_fsdp)
        c = lax.div(p, half)
        r = p * (1 - c) + (n_fsdp - 1 - p) * c
        return 2 * r + c

    ring_peer = (at(pos + 1), at(pos - 1))

    def shard_of(way, s):
        return at(pos - s) if way == 0 else at(pos + s)

    def piece(q, kind, p):
        if kind == 1:
            return weights.at[q, pl.ds(pl.multiple_of(4 * swapped + p * kept, 16), kept), :]
        return weights.at[q, pl.ds(pl.multiple_of(p * swapped, 16), swapped), :]

    own = (xbit * 2 + core, core)
    x_own = (1 - xbit) * 2 + core
    core_own = (xbit * 2 + 1 - core, 1 - core, (1 - xbit) * 2 + 1 - core)

    def remote(src, dst, send, recv, **where):
        return pltpu.make_async_remote_copy(
            src_ref=src, dst_ref=dst, send_sem=send, recv_sem=recv,
            device_id=where, device_id_type=MESH,
        )

    def ring_copy(way, s, kind, q):
        ref = piece(q, kind, own[kind])
        return remote(ref, ref, ring_s.at[way, s - 1, kind], ring_r.at[way, s - 1, kind], fsdp=ring_peer[way])

    def x_copy(way, s, q, p):
        ref = piece(q, 0, p)
        return remote(ref, ref, x_s.at[way, s - 1], x_r.at[way, s - 1], dp=x_peer)

    def core_copy(way, s, kind, q, p):
        ref = piece(q, kind, p)
        return remote(ref, ref, core_s.at[way, s - 1, kind], core_r.at[way, s - 1, kind], dp=core_peer)

    def has(way, s, kind):
        return s < half or (s == half and way == kind)

    value_copy = pltpu.make_async_copy(value_hbm, weights.at[me, pl.ds(0, rows), :], local_sem.at[0])
    hid_copy = pltpu.make_async_copy(hid_hbm, hid, local_sem.at[1])
    read_copy = pltpu.make_async_copy(read_hbm, read, local_sem.at[2])
    value_copy.start()
    hid_copy.start()
    read_copy.start()

    barrier = pltpu.get_barrier_semaphore()

    for where in ({"fsdp": ring_peer[0]}, {"fsdp": ring_peer[1]}, {"dp": x_peer}, {"dp": core_peer}):
        pl.semaphore_signal(barrier, inc=1, device_id=where, device_id_type=MESH)

    for t in range(groups // 2):
        pair = [down_ref[:, g * PACK:(g + 1) * PACK].astype(jnp.float32) for g in (2 * t, 2 * t + 1)]
        tile = jnp.transpose(jnp.concatenate(pair, axis=0)).astype(jnp.bfloat16)
        weights[me, rows:rows + PACK, t * LANES:(t + 1) * LANES] = tile
    used = groups // 2 * LANES
    if used < weights.shape[2]:
        weights[me, rows:rows + PACK, used:] = jnp.zeros((PACK, weights.shape[2] - used), jnp.bfloat16)

    value_copy.wait()
    pl.semaphore_wait(barrier, 4)

    for kind in (0, 1):
        for way in (0, 1):
            if has(way, 1, kind):
                ring_copy(way, 1, kind, me).start()

    def multiply(q):
        first = pl.multiple_of(q * rows, rows)
        base[...] += jnp.dot(
            hid[:, pl.ds(first, rows)], weights[q, 0:rows, :], preferred_element_type=jnp.float32
        )
        left, right = acc_l[...], acc_r[...]
        for t in range(groups // 2):
            tile = weights[q, rows:rows + PACK, t * LANES:(t + 1) * LANES]
            begin = pl.multiple_of(q * rows + 2 * t * PACK, PACK)
            left += jnp.dot(hid[:, pl.ds(begin, PACK)], tile, preferred_element_type=jnp.float32)
            begin = pl.multiple_of(q * rows + (2 * t + 1) * PACK, PACK)
            right += jnp.dot(hid[:, pl.ds(begin, PACK)], tile, preferred_element_type=jnp.float32)
        acc_l[...] = left
        acc_r[...] = right

    base[...] = jnp.zeros_like(base)
    acc_l[...] = jnp.zeros_like(acc_l)
    acc_r[...] = jnp.zeros_like(acc_r)
    hid_copy.wait()
    multiply(me)

    read_copy.wait()
    resp = resp_ref[...].astype(jnp.float32)
    masks = [
        jnp.transpose(jnp.broadcast_to(resp[i:i + 1, :], (seq, seq)))[:, 0:1] for i in (0, 1)
    ]
    weighted[...] = read[...].astype(jnp.float32) * jnp.concatenate(masks, axis=0)

    def take_ring(s, kind):
        for way in (0, 1):
            if has(way, s, kind):
                q = shard_of(way, s)
                ring_copy(way, s, kind, q).wait_recv()
                if has(way, s + 1, kind):
                    ring_copy(way, s + 1, kind, q).start()
                if kind == 0:
                    x_copy(way, s, q, own[0]).start()
                core_copy(way, s, kind, q, own[kind]).start()

    def take_x(s):
        for way in (0, 1):
            if has(way, s, 0):
                q = shard_of(way, s)
                x_copy(way, s, q, x_own).wait_recv()
                core_copy(way, s, 2, q, x_own).start()

    def finish(s):
        for way in (0, 1):
            for kind in (0, 1, 2):
                if has(way, s, kind % 2):
                    core_copy(way, s, kind, shard_of(way, s), core_own[kind]).wait_recv()
        if s == half:
            multiply(shard_of(0, s))
        else:
            def both(i, _):
                multiply(at(pos + s * (2 * i - 1)))
                return 0
            lax.fori_loop(0, 2, both, 0)

    for s in range(1, half + 1):
        take_ring(s, 0)
        if s > 1:
            take_x(s - 1)
        take_ring(s, 1)
        if s > 1:
            finish(s - 1)
    take_x(half)
    finish(half)

    low = (acc_l[:, 0:rank] + acc_r[:, rank:2 * rank]).astype(jnp.bfloat16)
    ref_act = base[...]
    policy = ref_act + ADAPTER_SCALE * jnp.dot(low, up_ref[...], preferred_element_type=jnp.float32)
    t_policy = jnp.tanh(policy)
    scores = weighted[...] * (t_policy - jnp.tanh(ref_act))
    diff = scores[0:seq, :] - scores[seq:, :]
    tile = jnp.zeros((seq, LANES), jnp.float32)
    for t in range(diff.shape[1] // LANES):
        tile += diff[:, t * LANES:(t + 1) * LANES]
    ratio_buf[me] = jnp.sum(tile.reshape(seq // 8, 8, LANES), axis=0)

    def ratio_copy(k):
        return remote(
            ratio_buf.at[me], ratio_buf.at[me], ratio_s.at[k], ratio_r.at[k], fsdp=lax.rem(me + k, n_fsdp)
        )

    def each(first, last, body):
        def step(k, _):
            body(k)
            return 0
        lax.fori_loop(first, last, step, 0)

    each(1, n_fsdp, lambda k: ratio_copy(k).start())
    slope = DPO_BETA * weighted[...] * (1.0 - t_policy * t_policy)
    grad_h = jnp.concatenate([-slope[0:seq, :], slope[seq:, :]], axis=0).astype(jnp.bfloat16)
    grad_low = ADAPTER_SCALE * lax.dot_general(
        grad_h, up_ref[...], (((1,), (1,)), ((), ())), preferred_element_type=jnp.float32
    )
    grad_low_t[...] = jnp.transpose(grad_low).astype(jnp.bfloat16)
    grad_b_t = ADAPTER_SCALE * lax.dot_general(
        grad_h, low, (((0,), (0,)), ((), ())), preferred_element_type=jnp.float32
    )
    for q in range(n_fsdp):
        block = grad_b_t[q * up_rows:(q + 1) * up_rows, :]
        block = jnp.concatenate([block, jnp.zeros((up_rows, LANES - rank), jnp.float32)], axis=1)
        if up_rows < rank:
            block = jnp.concatenate([block, jnp.zeros((rank - up_rows, LANES), jnp.float32)], axis=0)
        part[q, :, rows:rows + LANES] = block

    half_rows, quarter = rank // 2, rank // 4
    mine1 = pl.multiple_of(core * half_rows, half_rows)
    theirs1 = pl.multiple_of((1 - core) * half_rows, half_rows)

    def block_of(k):
        return lax.rem(me + k, n_fsdp)

    def copy1(k):
        return remote(
            part.at[block_of(k), pl.ds(theirs1, half_rows), :], buf1.at[k], s1.at[k], r1.at[k], dp=core_peer
        )

    def copy2(k):
        return remote(send2.at[k], buf2.at[k], s2.at[k], r2.at[k], dp=x_peer)

    def copy3(k):
        return remote(send3.at[k], buf3.at[k], s3.at[k], r3.at[k], fsdp=block_of(k))

    def stage1(k):
        q = block_of(k)
        part[q, :, 0:rows] = jnp.dot(
            grad_low_t[...], hid[:, pl.ds(pl.multiple_of(q * rows, rows), rows)],
            preferred_element_type=jnp.float32,
        )

    def stage2(k):
        q = block_of(k)
        copy1(k).wait_recv()
        give = pl.multiple_of((1 - xbit) * quarter, quarter)
        keep = pl.multiple_of(xbit * quarter, quarter)
        send2[k] = (part[q, pl.ds(mine1 + give, quarter), :] + buf1[k, pl.ds(give, quarter), :]).astype(jnp.bfloat16)
        copy2(k).start()
        total2[k] = part[q, pl.ds(mine1 + keep, quarter), :] + buf1[k, pl.ds(keep, quarter), :]

    def stage3(k):
        copy2(k).wait_recv()
        send3[k] = (total2[k] + buf2[k].astype(jnp.float32)).astype(jnp.bfloat16)
        copy3(k).start()

    def in_order(body, count=n_fsdp):
        def step(i):
            odd = lax.rem(i, 2)
            body(half + lax.div(i, 2) * (1 - odd) - lax.div(i + 1, 2) * odd)
        each(0, count, step)

    in_order(stage1)

    each(1, n_fsdp, lambda k: ratio_copy(k).wait())
    margin = DPO_BETA * jnp.sum(jnp.sum(ratio_buf[...], axis=0), keepdims=True)
    loss = jnp.maximum(-margin, 0.0) + jnp.log1p(jnp.exp(-jnp.abs(margin)))
    gate = 1.0 / (1.0 + jnp.exp(margin))

    def send1(k):
        q = block_of(k)
        part[q] = part[q] * gate
        copy1(k).start()

    in_order(send1)
    in_order(stage2)
    in_order(stage3, n_fsdp - 1)
    copy2(0).wait_recv()
    total2[0] = total2[0] + buf2[0].astype(jnp.float32)

    def stage4(k):
        copy3(k).wait_recv()
        total2[0] = total2[0] + buf3[k].astype(jnp.float32)

    in_order(stage4, n_fsdp - 1)
    final[0] = total2[0].astype(jnp.bfloat16)

    def copy4(k):
        return remote(final.at[0], final.at[k], s4.at[k], r4.at[k], dp=lax.rem(d + k, n_dp))

    each(1, n_dp, lambda k: copy4(k).start())

    for s in range(1, half + 1):
        for way in (0, 1):
            for kind in (0, 1):
                if has(way, s, kind):
                    ring_copy(way, s, kind, me).wait_send()
                    core_copy(way, s, kind, me, own[kind]).wait_send()
            if has(way, s, 0):
                x_copy(way, s, me, own[0]).wait_send()
                core_copy(way, s, 2, me, x_own).wait_send()
    each(0, n_fsdp, lambda k: copy1(k).wait_send())
    each(0, n_fsdp, lambda k: copy2(k).wait_send())
    each(1, n_fsdp, lambda k: copy3(k).wait_send())

    each(1, n_dp, lambda k: copy4(k).wait())
    for c in (0, 1):
        for x in (0, 1):
            begin = c * half_rows + x * quarter
            total = jnp.zeros((quarter, rows + LANES), jnp.float32)
            for h in range(n_dp // 4):
                slot = lax.rem(d - (h * 4 + x * 2 + c) + n_dp, n_dp)
                total += final[slot].astype(jnp.float32)
            out[begin:begin + quarter, :] = total
    wide = rows + LANES
    out[rank:rank + 8, :] = jnp.broadcast_to(loss, (8, wide))
    out[rank + 8:rank + 16, :] = jnp.broadcast_to(margin, (8, wide))


def unpack(joined, down_out, up_out, loss_out, margin_out):
    rank, rows = down_out.shape
    up_rows = up_out.shape[0]
    down_out[...] = joined[0:rank, 0:rows]
    up_out[...] = joined[0:up_rows, rows:rows + up_out.shape[1]]
    loss_out[0] = jnp.max(joined[rank:rank + 8, 0:LANES])
    margin_out[0] = jnp.max(joined[rank + 8:rank + 16, 0:LANES])


def shards(n_dp, n_fsdp, hidden_input, readout, response, value_matrix, adapter_down, adapter_up):
    seq = hidden_input.shape[2]
    tokens = 2 * seq
    model = hidden_input.shape[3]
    rows, features = value_matrix.shape
    rank = adapter_down.shape[1]
    half = n_fsdp // 2
    quarter = rank // 4
    wide = rows + LANES
    f32, bf16 = jnp.float32, jnp.bfloat16
    vmem = pl.BlockSpec(memory_space=pltpu.VMEM)
    hbm = pl.BlockSpec(memory_space=pl.ANY)
    dma = pltpu.SemaphoreType.DMA
    joined = pl.pallas_call(
        functools.partial(kernel, n_dp, n_fsdp),
        out_shape=jax.ShapeDtypeStruct((rank + 16, wide), f32),
        in_specs=[hbm, hbm, vmem, hbm, vmem, vmem],
        out_specs=vmem,
        scratch_shapes=[
            pltpu.VMEM((tokens, model), bf16),
            pltpu.VMEM((tokens, features), bf16),
            pltpu.VMEM((tokens, features), f32),
            pltpu.VMEM((n_fsdp, rows + PACK, features), bf16),
            pltpu.VMEM((tokens, features), f32),
            pltpu.VMEM((tokens, LANES), f32),
            pltpu.VMEM((tokens, LANES), f32),
            pltpu.VMEM((rank, tokens), bf16),
            pltpu.VMEM((n_fsdp, 8, LANES), f32),
            pltpu.VMEM((n_fsdp, rank, wide), f32),
            pltpu.VMEM((n_fsdp, rank // 2, wide), f32),
            pltpu.VMEM((n_fsdp, quarter, wide), bf16),
            pltpu.VMEM((n_fsdp, quarter, wide), bf16),
            pltpu.VMEM((n_fsdp, quarter, wide), f32),
            pltpu.VMEM((n_fsdp, quarter, wide), bf16),
            pltpu.VMEM((n_fsdp, quarter, wide), bf16),
            pltpu.VMEM((n_dp, quarter, wide), bf16),
            dma((3,)),
            dma((2, half, 2)), dma((2, half, 2)),
            dma((2, half)), dma((2, half)),
            dma((2, half, 3)), dma((2, half, 3)),
            dma((n_fsdp,)), dma((n_fsdp,)),
            dma((n_fsdp,)), dma((n_fsdp,)),
            dma((n_fsdp,)), dma((n_fsdp,)),
            dma((n_fsdp,)), dma((n_fsdp,)),
            dma((n_dp,)), dma((n_dp,)),
        ],
        compiler_params=pltpu.CompilerParams(
            collective_id=0, has_side_effects=True, vmem_limit_bytes=56 << 20
        ),
        name="dpo_adapter_gradient",
    )(
        hidden_input.reshape(tokens, model),
        readout.reshape(tokens, features),
        response.reshape(2, seq),
        value_matrix,
        adapter_down.T,
        adapter_up,
    )
    smem = pl.BlockSpec(memory_space=pltpu.SMEM)
    down_t, up_block, loss, margin = pl.pallas_call(
        unpack,
        out_shape=(
            jax.ShapeDtypeStruct((rank, rows), f32),
            jax.ShapeDtypeStruct((features // n_fsdp, rank), f32),
            jax.ShapeDtypeStruct((1,), f32),
            jax.ShapeDtypeStruct((1,), f32),
        ),
        in_specs=[vmem],
        out_specs=(vmem, vmem, smem, smem),
        name="unpack_gradients",
    )(joined)
    return down_t.T, up_block, loss, margin


def solution(mesh):
    placed = (
        P("dp", None, "fsdp", None),
        P("dp", None, "fsdp", None),
        P("dp", None, "fsdp"),
        P("fsdp", None),
        P("fsdp", None),
        P(),
    )
    return jax.shard_map(
        functools.partial(shards, mesh.shape["dp"], mesh.shape["fsdp"]),
        mesh=mesh,
        in_specs=placed,
        out_specs=(P("fsdp", None), P("fsdp", None), P("dp"), P("dp")),
        check_vma=False,
    )
```

```python
import functools

import jax
import jax.numpy as jnp
from jax import lax
from jax.experimental import pallas as pl
from jax.experimental.pallas import tpu as pltpu
from jax.sharding import PartitionSpec as P

DPO_BETA = 0.5
ADAPTER_SCALE = 2.0
LANES = 128
PACK = 128
MESH = pl.DeviceIdType.MESH


def kernel(
    n_dp, n_fsdp,
    hid_hbm, read_hbm, resp_ref, value_hbm, down_ref, up_ref,
    out,
    hid, read, weighted, weights, base, acc, spread, grad_low_t,
    ratio_buf, part, buf1, send2, buf2, total2, send3, buf3, final,
    local_sem, ring_s, ring_r, x_s, x_r, core_s, core_r,
    ratio_s, ratio_r, s1, r1, s2, r2, s3, r3, s4, r4,
):
    half = n_fsdp // 2
    rows = value_hbm.shape[0]
    rank = down_ref.shape[0]
    tokens = hid.shape[0]
    seq = tokens // 2
    swapped = weights.shape[1] * 11 // 72 // 16 * 16
    kept = (weights.shape[1] - 4 * swapped) // 2
    groups = rows // PACK
    up_rows = base.shape[1] // n_fsdp

    me = lax.axis_index("fsdp")
    d = lax.axis_index("dp")
    core = lax.rem(d, 2)
    xbit = lax.rem(lax.div(d, 2), 2)
    core_peer = d + 1 - 2 * core
    x_peer = d + 2 - 4 * xbit

    col, row = lax.rem(me, 2), lax.div(me, 2)
    pos = row * (1 - col) + (n_fsdp - 1 - row) * col

    def at(p):
        p = lax.rem(p + 2 * n_fsdp, n_fsdp)
        c = lax.div(p, half)
        r = p * (1 - c) + (n_fsdp - 1 - p) * c
        return 2 * r + c

    ring_peer = (at(pos + 1), at(pos - 1))

    def shard_of(way, s):
        return at(pos - s) if way == 0 else at(pos + s)

    def piece(q, kind, p):
        if kind == 1:
            return weights.at[q, pl.ds(pl.multiple_of(4 * swapped + p * kept, 16), kept), :]
        return weights.at[q, pl.ds(pl.multiple_of(p * swapped, 16), swapped), :]

    own = (xbit * 2 + core, core)
    x_own = (1 - xbit) * 2 + core
    core_own = (xbit * 2 + 1 - core, 1 - core, (1 - xbit) * 2 + 1 - core)

    def remote(src, dst, send, recv, **where):
        return pltpu.make_async_remote_copy(
            src_ref=src, dst_ref=dst, send_sem=send, recv_sem=recv,
            device_id=where, device_id_type=MESH,
        )

    def ring_copy(way, s, kind, q):
        ref = piece(q, kind, own[kind])
        return remote(ref, ref, ring_s.at[way, s - 1, kind], ring_r.at[way, s - 1, kind], fsdp=ring_peer[way])

    def x_copy(way, s, q, p):
        ref = piece(q, 0, p)
        return remote(ref, ref, x_s.at[way, s - 1], x_r.at[way, s - 1], dp=x_peer)

    def core_copy(way, s, kind, q, p):
        ref = piece(q, kind, p)
        return remote(ref, ref, core_s.at[way, s - 1, kind], core_r.at[way, s - 1, kind], dp=core_peer)

    def has(way, s, kind):
        return s < half or (s == half and way == kind)

    value_copy = pltpu.make_async_copy(value_hbm, weights.at[me, pl.ds(0, rows), :], local_sem.at[0])
    hid_copy = pltpu.make_async_copy(hid_hbm, hid, local_sem.at[1])
    read_copy = pltpu.make_async_copy(read_hbm, read, local_sem.at[2])
    value_copy.start()
    hid_copy.start()
    read_copy.start()

    barrier = pltpu.get_barrier_semaphore()

    greeted = [{"fsdp": ring_peer[0]}, {"fsdp": ring_peer[1]}]
    if n_dp == 4:
        greeted += [{"dp": x_peer}, {"dp": core_peer}]
    else:
        greeted += [{"dp": lax.rem(d + k, n_dp)} for k in range(1, n_dp)]
    for where in greeted:
        pl.semaphore_signal(barrier, inc=1, device_id=where, device_id_type=MESH)

    for t in range(groups // 2):
        pair = [down_ref[:, g * PACK:(g + 1) * PACK].astype(jnp.float32) for g in (2 * t, 2 * t + 1)]
        tile = jnp.transpose(jnp.concatenate(pair, axis=0)).astype(jnp.bfloat16)
        weights[me, rows:rows + PACK, t * LANES:(t + 1) * LANES] = tile
    used = groups // 2 * LANES
    if used < weights.shape[2]:
        weights[me, rows:rows + PACK, used:] = jnp.zeros((PACK, weights.shape[2] - used), jnp.bfloat16)

    value_copy.wait()
    pl.semaphore_wait(barrier, len(greeted))

    for kind in (0, 1):
        for way in (0, 1):
            if has(way, 1, kind):
                ring_copy(way, 1, kind, me).start()

    in_left = lax.broadcasted_iota(jnp.int32, (PACK, LANES), 1) < rank

    def multiply(q):
        first = pl.multiple_of(q * rows, rows)
        base[...] += jnp.dot(
            hid[:, pl.ds(first, rows)], weights[q, 0:rows, :], preferred_element_type=jnp.float32
        )
        for t in range(groups // 2):
            tile = weights[q, rows:rows + PACK, t * LANES:(t + 1) * LANES]
            zero = jnp.zeros_like(tile)
            spread[2 * t * PACK:(2 * t + 1) * PACK, :] = jnp.where(in_left, tile, zero)
            spread[(2 * t + 1) * PACK:(2 * t + 2) * PACK, :] = jnp.where(in_left, zero, tile)
        acc[...] += jnp.dot(hid[:, pl.ds(first, rows)], spread[...], preferred_element_type=jnp.float32)

    base[...] = jnp.zeros_like(base)
    acc[...] = jnp.zeros_like(acc)
    hid_copy.wait()
    multiply(me)

    read_copy.wait()
    resp = resp_ref[...].astype(jnp.float32)
    masks = [
        jnp.transpose(jnp.broadcast_to(resp[i:i + 1, :], (seq, seq)))[:, 0:1] for i in (0, 1)
    ]
    weighted[...] = read[...].astype(jnp.float32) * jnp.concatenate(masks, axis=0)

    def take_ring(s, kind):
        for way in (0, 1):
            if has(way, s, kind):
                q = shard_of(way, s)
                ring_copy(way, s, kind, q).wait_recv()
                if has(way, s + 1, kind):
                    ring_copy(way, s + 1, kind, q).start()
                if kind == 0:
                    x_copy(way, s, q, own[0]).start()
                core_copy(way, s, kind, q, own[kind]).start()

    def take_x(s):
        for way in (0, 1):
            if has(way, s, 0):
                q = shard_of(way, s)
                x_copy(way, s, q, x_own).wait_recv()
                core_copy(way, s, 2, q, x_own).start()

    def take_core(way, s):
        for kind in (0, 1, 2):
            if has(way, s, kind % 2):
                core_copy(way, s, kind, shard_of(way, s), core_own[kind]).wait_recv()

    def finish(way, s):
        take_core(way, s)
        multiply(shard_of(way, s))

    for s in range(1, half):
        take_ring(s, 0)
        if s > 1:
            take_x(s - 1)
        take_ring(s, 1)
        if s > 1:
            finish(0, s - 1)
            finish(1, s - 1)
    take_x(half - 1)
    finish(1, half - 1)
    take_ring(half, 0)
    take_ring(half, 1)
    finish(0, half - 1)
    take_x(half)
    take_core(0, half)
    finish(1, half)

    low = (acc[:, 0:rank] + acc[:, rank:2 * rank]).astype(jnp.bfloat16)
    ref_act = base[...]
    policy = ref_act + ADAPTER_SCALE * jnp.dot(low, up_ref[...], preferred_element_type=jnp.float32)
    t_policy = jnp.tanh(policy)
    scores = weighted[...] * (t_policy - jnp.tanh(ref_act))
    diff = scores[0:seq, :] - scores[seq:, :]
    tile = jnp.zeros((seq, LANES), jnp.float32)
    for t in range(diff.shape[1] // LANES):
        tile += diff[:, t * LANES:(t + 1) * LANES]
    ratio_buf[me] = jnp.sum(tile.reshape(seq // 8, 8, LANES), axis=0)

    def ratio_copy(k):
        return remote(
            ratio_buf.at[me], ratio_buf.at[me], ratio_s.at[k], ratio_r.at[k], fsdp=lax.rem(me + k, n_fsdp)
        )

    def each(first, last, body):
        def step(k, _):
            body(k)
            return 0
        lax.fori_loop(first, last, step, 0)

    each(1, n_fsdp, lambda k: ratio_copy(k).start())
    slope = DPO_BETA * weighted[...] * (1.0 - t_policy * t_policy)
    grad_h = jnp.concatenate([-slope[0:seq, :], slope[seq:, :]], axis=0).astype(jnp.bfloat16)
    grad_low = ADAPTER_SCALE * lax.dot_general(
        grad_h, up_ref[...], (((1,), (1,)), ((), ())), preferred_element_type=jnp.float32
    )
    grad_low_t[...] = jnp.transpose(grad_low).astype(jnp.bfloat16)
    grad_b_t = ADAPTER_SCALE * lax.dot_general(
        grad_h, low, (((0,), (0,)), ((), ())), preferred_element_type=jnp.float32
    )
    for q in range(n_fsdp):
        block = grad_b_t[q * up_rows:(q + 1) * up_rows, :]
        block = jnp.concatenate([block, jnp.zeros((up_rows, LANES - rank), jnp.float32)], axis=1)
        if up_rows < rank:
            block = jnp.concatenate([block, jnp.zeros((rank - up_rows, LANES), jnp.float32)], axis=0)
        part[q, :, rows:rows + LANES] = block

    half_rows, quarter = rank // 2, rank // 4
    mine1 = pl.multiple_of(core * half_rows, half_rows)
    theirs1 = pl.multiple_of((1 - core) * half_rows, half_rows)

    def block_of(k):
        return lax.rem(me + k, n_fsdp)

    def copy1(k):
        return remote(
            part.at[block_of(k), pl.ds(theirs1, half_rows), :], buf1.at[k], s1.at[k], r1.at[k], dp=core_peer
        )

    def copy2(k):
        return remote(send2.at[k], buf2.at[k], s2.at[k], r2.at[k], dp=x_peer)

    def copy3(k):
        return remote(send3.at[k], buf3.at[k], s3.at[k], r3.at[k], fsdp=block_of(k))

    def stage1(k):
        q = block_of(k)
        part[q, :, 0:rows] = jnp.dot(
            grad_low_t[...], hid[:, pl.ds(pl.multiple_of(q * rows, rows), rows)],
            preferred_element_type=jnp.float32,
        )

    def stage2(k):
        q = block_of(k)
        copy1(k).wait_recv()
        give = pl.multiple_of((1 - xbit) * quarter, quarter)
        keep = pl.multiple_of(xbit * quarter, quarter)
        send2[k] = (part[q, pl.ds(mine1 + give, quarter), :] + buf1[k, pl.ds(give, quarter), :]).astype(jnp.bfloat16)
        copy2(k).start()
        total2[k] = part[q, pl.ds(mine1 + keep, quarter), :] + buf1[k, pl.ds(keep, quarter), :]

    def stage3(k):
        copy2(k).wait_recv()
        send3[k] = (total2[k] + buf2[k].astype(jnp.float32)).astype(jnp.bfloat16)
        copy3(k).start()

    def in_order(body, count=n_fsdp, begin=0):
        def step(i):
            odd = lax.rem(i, 2)
            body(half + lax.div(i, 2) * (1 - odd) - lax.div(i + 1, 2) * odd)
        each(begin, count, step)

    in_order(stage1, half)

    each(1, n_fsdp, lambda k: ratio_copy(k).wait())
    margin = DPO_BETA * jnp.sum(jnp.sum(ratio_buf[...], axis=0), keepdims=True)
    loss = jnp.maximum(-margin, 0.0) + jnp.log1p(jnp.exp(-jnp.abs(margin)))
    gate = 1.0 / (1.0 + jnp.exp(margin))

    def send1(k):
        q = block_of(k)
        part[q] = part[q] * gate
        copy1(k).start()

    def both1(k):
        stage1(k)
        send1(k)

    in_order(send1, half)
    in_order(both1, n_fsdp, half)
    in_order(stage2)
    in_order(stage3, n_fsdp - 1)
    copy2(0).wait_recv()
    total2[0] = total2[0] + buf2[0].astype(jnp.float32)

    def stage4(k):
        copy3(k).wait_recv()
        total2[0] = total2[0] + buf3[k].astype(jnp.float32)

    in_order(stage4, n_fsdp - 1)
    final[0] = total2[0].astype(jnp.bfloat16)

    def copy4(k):
        return remote(final.at[0], final.at[k], s4.at[k], r4.at[k], dp=lax.rem(d + k, n_dp))

    each(1, n_dp, lambda k: copy4(k).start())

    for s in range(1, half + 1):
        for way in (0, 1):
            for kind in (0, 1):
                if has(way, s, kind):
                    ring_copy(way, s, kind, me).wait_send()
                    core_copy(way, s, kind, me, own[kind]).wait_send()
            if has(way, s, 0):
                x_copy(way, s, me, own[0]).wait_send()
                core_copy(way, s, 2, me, x_own).wait_send()
    each(0, n_fsdp, lambda k: copy1(k).wait_send())
    each(0, n_fsdp, lambda k: copy2(k).wait_send())
    each(1, n_fsdp, lambda k: copy3(k).wait_send())

    each(1, n_dp, lambda k: copy4(k).wait())
    for c in (0, 1):
        for x in (0, 1):
            begin = c * half_rows + x * quarter
            total = jnp.zeros((quarter, rows + LANES), jnp.float32)
            for h in range(n_dp // 4):
                slot = lax.rem(d - (h * 4 + x * 2 + c) + n_dp, n_dp)
                total += final[slot].astype(jnp.float32)
            out[begin:begin + quarter, :] = total
    wide = rows + LANES
    out[rank:rank + 8, :] = jnp.broadcast_to(loss, (8, wide))
    out[rank + 8:rank + 16, :] = jnp.broadcast_to(margin, (8, wide))


def unpack(joined, down_out, up_out, loss_out, margin_out):
    rank, rows = down_out.shape
    up_rows = up_out.shape[0]
    down_out[...] = joined[0:rank, 0:rows]
    up_out[...] = joined[0:up_rows, rows:rows + up_out.shape[1]]
    loss_out[0] = jnp.max(joined[rank:rank + 8, 0:LANES])
    margin_out[0] = jnp.max(joined[rank + 8:rank + 16, 0:LANES])


def shards(n_dp, n_fsdp, hidden_input, readout, response, value_matrix, adapter_down, adapter_up):
    seq = hidden_input.shape[2]
    tokens = 2 * seq
    model = hidden_input.shape[3]
    rows, features = value_matrix.shape
    rank = adapter_down.shape[1]
    half = n_fsdp // 2
    quarter = rank // 4
    wide = rows + LANES
    f32, bf16 = jnp.float32, jnp.bfloat16
    vmem = pl.BlockSpec(memory_space=pltpu.VMEM)
    hbm = pl.BlockSpec(memory_space=pl.ANY)
    dma = pltpu.SemaphoreType.DMA
    joined = pl.pallas_call(
        functools.partial(kernel, n_dp, n_fsdp),
        out_shape=jax.ShapeDtypeStruct((rank + 16, wide), f32),
        in_specs=[hbm, hbm, vmem, hbm, vmem, vmem],
        out_specs=vmem,
        scratch_shapes=[
            pltpu.VMEM((tokens, model), bf16),
            pltpu.VMEM((tokens, features), bf16),
            pltpu.VMEM((tokens, features), f32),
            pltpu.VMEM((n_fsdp, rows + PACK, features), bf16),
            pltpu.VMEM((tokens, features), f32),
            pltpu.VMEM((tokens, LANES), f32),
            pltpu.VMEM((rows, LANES), bf16),
            pltpu.VMEM((rank, tokens), bf16),
            pltpu.VMEM((n_fsdp, 8, LANES), f32),
            pltpu.VMEM((n_fsdp, rank, wide), f32),
            pltpu.VMEM((n_fsdp, rank // 2, wide), f32),
            pltpu.VMEM((n_fsdp, quarter, wide), bf16),
            pltpu.VMEM((n_fsdp, quarter, wide), bf16),
            pltpu.VMEM((n_fsdp, quarter, wide), f32),
            pltpu.VMEM((n_fsdp, quarter, wide), bf16),
            pltpu.VMEM((n_fsdp, quarter, wide), bf16),
            pltpu.VMEM((n_dp, quarter, wide), bf16),
            dma((3,)),
            dma((2, half, 2)), dma((2, half, 2)),
            dma((2, half)), dma((2, half)),
            dma((2, half, 3)), dma((2, half, 3)),
            dma((n_fsdp,)), dma((n_fsdp,)),
            dma((n_fsdp,)), dma((n_fsdp,)),
            dma((n_fsdp,)), dma((n_fsdp,)),
            dma((n_fsdp,)), dma((n_fsdp,)),
            dma((n_dp,)), dma((n_dp,)),
        ],
        compiler_params=pltpu.CompilerParams(
            collective_id=0, has_side_effects=True, vmem_limit_bytes=56 << 20
        ),
        name="dpo_adapter_gradient",
    )(
        hidden_input.reshape(tokens, model),
        readout.reshape(tokens, features),
        response.reshape(2, seq),
        value_matrix,
        adapter_down.T,
        adapter_up,
    )
    smem = pl.BlockSpec(memory_space=pltpu.SMEM)
    down_t, up_block, loss, margin = pl.pallas_call(
        unpack,
        out_shape=(
            jax.ShapeDtypeStruct((rank, rows), f32),
            jax.ShapeDtypeStruct((features // n_fsdp, rank), f32),
            jax.ShapeDtypeStruct((1,), f32),
            jax.ShapeDtypeStruct((1,), f32),
        ),
        in_specs=[vmem],
        out_specs=(vmem, vmem, smem, smem),
        name="unpack_gradients",
    )(joined)
    return down_t.T, up_block, loss, margin


def solution(mesh):
    placed = (
        P("dp", None, "fsdp", None),
        P("dp", None, "fsdp", None),
        P("dp", None, "fsdp"),
        P("fsdp", None),
        P("fsdp", None),
        P(),
    )
    return jax.shard_map(
        functools.partial(shards, mesh.shape["dp"], mesh.shape["fsdp"]),
        mesh=mesh,
        in_specs=placed,
        out_specs=(P("fsdp", None), P("fsdp", None), P("dp"), P("dp")),
        check_vma=False,
    )
```

```python
import functools

import jax
import jax.numpy as jnp
from jax import lax
from jax.experimental import pallas as pl
from jax.experimental.pallas import tpu as pltpu
from jax.sharding import PartitionSpec as P

DPO_BETA = 0.5
ADAPTER_SCALE = 2.0
LANES = 128
PACK = 128
MESH = pl.DeviceIdType.MESH


def kernel(
    n_dp, n_fsdp,
    hid_hbm, read_hbm, resp_ref, value_hbm, down_ref, up_ref,
    out,
    hid, read, weighted, weights, base, acc, spread, grad_low_t,
    ratio_buf, part, buf1, send2, buf2, total2, send3, buf3, final,
    local_sem, ring_s, ring_r, x_s, x_r, core_s, core_r,
    ratio_s, ratio_r, s1, r1, s2, r2, s3, r3, s4, r4,
):
    half = n_fsdp // 2
    rows = value_hbm.shape[0]
    rank = down_ref.shape[0]
    tokens = hid.shape[0]
    seq = tokens // 2
    swapped = weights.shape[1] * 10 // 72 // 16 * 16
    kept = (weights.shape[1] - 4 * swapped) // 2
    groups = rows // PACK
    up_rows = base.shape[1] // n_fsdp

    me = lax.axis_index("fsdp")
    d = lax.axis_index("dp")
    core = lax.rem(d, 2)
    xbit = lax.rem(lax.div(d, 2), 2)
    core_peer = d + 1 - 2 * core
    x_peer = d + 2 - 4 * xbit

    col, row = lax.rem(me, 2), lax.div(me, 2)
    pos = row * (1 - col) + (n_fsdp - 1 - row) * col

    def at(p):
        p = lax.rem(p + 2 * n_fsdp, n_fsdp)
        c = lax.div(p, half)
        r = p * (1 - c) + (n_fsdp - 1 - p) * c
        return 2 * r + c

    ring_peer = (at(pos + 1), at(pos - 1))

    def shard_of(way, s):
        return at(pos - s) if way == 0 else at(pos + s)

    def piece(q, kind, p):
        if kind == 1:
            return weights.at[q, pl.ds(pl.multiple_of(4 * swapped + p * kept, 16), kept), :]
        return weights.at[q, pl.ds(pl.multiple_of(p * swapped, 16), swapped), :]

    own = (xbit * 2 + core, core)
    x_own = (1 - xbit) * 2 + core
    core_own = (xbit * 2 + 1 - core, 1 - core, (1 - xbit) * 2 + 1 - core)

    def remote(src, dst, send, recv, **where):
        return pltpu.make_async_remote_copy(
            src_ref=src, dst_ref=dst, send_sem=send, recv_sem=recv,
            device_id=where, device_id_type=MESH,
        )

    def ring_copy(way, s, kind, q):
        ref = piece(q, kind, own[kind])
        return remote(ref, ref, ring_s.at[way, s - 1, kind], ring_r.at[way, s - 1, kind], fsdp=ring_peer[way])

    def x_copy(way, s, q, p):
        ref = piece(q, 0, p)
        return remote(ref, ref, x_s.at[way, s - 1], x_r.at[way, s - 1], dp=x_peer)

    def core_copy(way, s, kind, q, p):
        ref = piece(q, kind, p)
        return remote(ref, ref, core_s.at[way, s - 1, kind], core_r.at[way, s - 1, kind], dp=core_peer)

    def has(way, s, kind):
        return s < half or (s == half and way == kind)

    value_copy = pltpu.make_async_copy(value_hbm, weights.at[me, pl.ds(0, rows), :], local_sem.at[0])
    hid_copy = pltpu.make_async_copy(hid_hbm, hid, local_sem.at[1])
    read_copy = pltpu.make_async_copy(read_hbm, read, local_sem.at[2])
    value_copy.start()
    hid_copy.start()
    read_copy.start()

    barrier = pltpu.get_barrier_semaphore()

    greeted = [{"fsdp": ring_peer[0]}, {"fsdp": ring_peer[1]}]
    if n_dp == 4:
        greeted += [{"dp": x_peer}, {"dp": core_peer}]
    else:
        greeted += [{"dp": lax.rem(d + k, n_dp)} for k in range(1, n_dp)]
    for where in greeted:
        pl.semaphore_signal(barrier, inc=1, device_id=where, device_id_type=MESH)

    for t in range(groups // 2):
        pair = [down_ref[:, g * PACK:(g + 1) * PACK].astype(jnp.float32) for g in (2 * t, 2 * t + 1)]
        tile = jnp.transpose(jnp.concatenate(pair, axis=0)).astype(jnp.bfloat16)
        weights[me, rows:rows + PACK, t * LANES:(t + 1) * LANES] = tile
    used = groups // 2 * LANES
    if used < weights.shape[2]:
        weights[me, rows:rows + PACK, used:] = jnp.zeros((PACK, weights.shape[2] - used), jnp.bfloat16)

    value_copy.wait()
    pl.semaphore_wait(barrier, len(greeted))

    for kind in (0, 1):
        for way in (0, 1):
            if has(way, 1, kind):
                ring_copy(way, 1, kind, me).start()

    in_left = lax.broadcasted_iota(jnp.int32, (PACK, LANES), 1) < rank

    def multiply(q):
        first = pl.multiple_of(q * rows, rows)
        base[...] += jnp.dot(
            hid[:, pl.ds(first, rows)], weights[q, 0:rows, :], preferred_element_type=jnp.float32
        )
        for t in range(groups // 2):
            tile = weights[q, rows:rows + PACK, t * LANES:(t + 1) * LANES]
            zero = jnp.zeros_like(tile)
            spread[2 * t * PACK:(2 * t + 1) * PACK, :] = jnp.where(in_left, tile, zero)
            spread[(2 * t + 1) * PACK:(2 * t + 2) * PACK, :] = jnp.where(in_left, zero, tile)
        acc[...] += jnp.dot(hid[:, pl.ds(first, rows)], spread[...], preferred_element_type=jnp.float32)

    base[...] = jnp.zeros_like(base)
    acc[...] = jnp.zeros_like(acc)
    hid_copy.wait()
    multiply(me)

    read_copy.wait()
    resp = resp_ref[...].astype(jnp.float32)
    masks = [
        jnp.transpose(jnp.broadcast_to(resp[i:i + 1, :], (seq, seq)))[:, 0:1] for i in (0, 1)
    ]
    weighted[...] = read[...].astype(jnp.float32) * jnp.concatenate(masks, axis=0)

    def take_ring(s, kind):
        for way in (0, 1):
            if has(way, s, kind):
                q = shard_of(way, s)
                ring_copy(way, s, kind, q).wait_recv()
                if has(way, s + 1, kind):
                    ring_copy(way, s + 1, kind, q).start()
                if kind == 0:
                    x_copy(way, s, q, own[0]).start()
                core_copy(way, s, kind, q, own[kind]).start()

    def take_x(s):
        for way in (0, 1):
            if has(way, s, 0):
                q = shard_of(way, s)
                x_copy(way, s, q, x_own).wait_recv()
                core_copy(way, s, 2, q, x_own).start()

    def take_core(way, s):
        for kind in (0, 1, 2):
            if has(way, s, kind % 2):
                core_copy(way, s, kind, shard_of(way, s), core_own[kind]).wait_recv()

    def finish(way, s):
        take_core(way, s)
        multiply(shard_of(way, s))

    for s in range(1, half + 1):
        take_ring(s, 0)
        if s > 1:
            take_x(s - 1)
        take_ring(s, 1)
        if s > 1:
            finish(0, s - 1)
            finish(1, s - 1)
    take_x(half)
    take_core(0, half)
    finish(1, half)

    low = (acc[:, 0:rank] + acc[:, rank:2 * rank]).astype(jnp.bfloat16)
    ref_act = base[...]
    policy = ref_act + ADAPTER_SCALE * jnp.dot(low, up_ref[...], preferred_element_type=jnp.float32)
    t_policy = jnp.tanh(policy)
    scores = weighted[...] * (t_policy - jnp.tanh(ref_act))
    diff = scores[0:seq, :] - scores[seq:, :]
    tile = jnp.zeros((seq, LANES), jnp.float32)
    for t in range(diff.shape[1] // LANES):
        tile += diff[:, t * LANES:(t + 1) * LANES]
    ratio_buf[me] = jnp.sum(tile.reshape(seq // 8, 8, LANES), axis=0)

    def ratio_copy(k):
        return remote(
            ratio_buf.at[me], ratio_buf.at[me], ratio_s.at[k], ratio_r.at[k], fsdp=lax.rem(me + k, n_fsdp)
        )

    def each(first, last, body):
        def step(k, _):
            body(k)
            return 0
        lax.fori_loop(first, last, step, 0)

    each(1, n_fsdp, lambda k: ratio_copy(k).start())
    slope = DPO_BETA * weighted[...] * (1.0 - t_policy * t_policy)
    grad_h = jnp.concatenate([-slope[0:seq, :], slope[seq:, :]], axis=0).astype(jnp.bfloat16)
    grad_low = ADAPTER_SCALE * lax.dot_general(
        grad_h, up_ref[...], (((1,), (1,)), ((), ())), preferred_element_type=jnp.float32
    )
    grad_low_t[...] = jnp.transpose(grad_low).astype(jnp.bfloat16)
    grad_b_t = ADAPTER_SCALE * lax.dot_general(
        grad_h, low, (((0,), (0,)), ((), ())), preferred_element_type=jnp.float32
    )
    for q in range(n_fsdp):
        block = grad_b_t[q * up_rows:(q + 1) * up_rows, :]
        block = jnp.concatenate([block, jnp.zeros((up_rows, LANES - rank), jnp.float32)], axis=1)
        if up_rows < rank:
            block = jnp.concatenate([block, jnp.zeros((rank - up_rows, LANES), jnp.float32)], axis=0)
        part[q, :, rows:rows + LANES] = block

    half_rows, quarter = rank // 2, rank // 4
    mine1 = pl.multiple_of(core * half_rows, half_rows)
    theirs1 = pl.multiple_of((1 - core) * half_rows, half_rows)

    def block_of(k):
        return lax.rem(me + k, n_fsdp)

    def copy1(k):
        return remote(
            part.at[block_of(k), pl.ds(theirs1, half_rows), :], buf1.at[k], s1.at[k], r1.at[k], dp=core_peer
        )

    def copy2(k):
        return remote(send2.at[k], buf2.at[k], s2.at[k], r2.at[k], dp=x_peer)

    def copy3(k):
        return remote(send3.at[k], buf3.at[k], s3.at[k], r3.at[k], fsdp=block_of(k))

    def stage1(k):
        q = block_of(k)
        part[q, :, 0:rows] = jnp.dot(
            grad_low_t[...], hid[:, pl.ds(pl.multiple_of(q * rows, rows), rows)],
            preferred_element_type=jnp.float32,
        )

    def stage2(k):
        q = block_of(k)
        copy1(k).wait_recv()
        give = pl.multiple_of((1 - xbit) * quarter, quarter)
        keep = pl.multiple_of(xbit * quarter, quarter)
        send2[k] = (part[q, pl.ds(mine1 + give, quarter), :] + buf1[k, pl.ds(give, quarter), :]).astype(jnp.bfloat16)
        copy2(k).start()
        total2[k] = part[q, pl.ds(mine1 + keep, quarter), :] + buf1[k, pl.ds(keep, quarter), :]

    def stage3(k):
        copy2(k).wait_recv()
        send3[k] = (total2[k] + buf2[k].astype(jnp.float32)).astype(jnp.bfloat16)
        copy3(k).start()

    def in_order(body, count=n_fsdp, begin=0):
        def step(i):
            odd = lax.rem(i, 2)
            body(half + lax.div(i, 2) * (1 - odd) - lax.div(i + 1, 2) * odd)
        each(begin, count, step)

    in_order(stage1, half)

    each(1, n_fsdp, lambda k: ratio_copy(k).wait())
    margin = DPO_BETA * jnp.sum(jnp.sum(ratio_buf[...], axis=0), keepdims=True)
    loss = jnp.maximum(-margin, 0.0) + jnp.log1p(jnp.exp(-jnp.abs(margin)))
    gate = 1.0 / (1.0 + jnp.exp(margin))

    def send1(k):
        q = block_of(k)
        part[q] = part[q] * gate
        copy1(k).start()

    def both1(k):
        stage1(k)
        send1(k)

    in_order(send1, half)
    in_order(both1, n_fsdp, half)
    in_order(stage2)
    in_order(stage3, n_fsdp - 1)
    copy2(0).wait_recv()
    total2[0] = total2[0] + buf2[0].astype(jnp.float32)

    def stage4(k):
        copy3(k).wait_recv()
        total2[0] = total2[0] + buf3[k].astype(jnp.float32)

    in_order(stage4, n_fsdp - 1)
    final[0] = total2[0].astype(jnp.bfloat16)

    def copy4(k):
        return remote(final.at[0], final.at[k], s4.at[k], r4.at[k], dp=lax.rem(d + k, n_dp))

    each(1, n_dp, lambda k: copy4(k).start())

    for s in range(1, half + 1):
        for way in (0, 1):
            for kind in (0, 1):
                if has(way, s, kind):
                    ring_copy(way, s, kind, me).wait_send()
                    core_copy(way, s, kind, me, own[kind]).wait_send()
            if has(way, s, 0):
                x_copy(way, s, me, own[0]).wait_send()
                core_copy(way, s, 2, me, x_own).wait_send()
    each(0, n_fsdp, lambda k: copy1(k).wait_send())
    each(0, n_fsdp, lambda k: copy2(k).wait_send())
    each(1, n_fsdp, lambda k: copy3(k).wait_send())

    each(1, n_dp, lambda k: copy4(k).wait())
    for c in (0, 1):
        for x in (0, 1):
            begin = c * half_rows + x * quarter
            total = jnp.zeros((quarter, rows + LANES), jnp.float32)
            for h in range(n_dp // 4):
                slot = lax.rem(d - (h * 4 + x * 2 + c) + n_dp, n_dp)
                total += final[slot].astype(jnp.float32)
            out[begin:begin + quarter, :] = total
    wide = rows + LANES
    out[rank:rank + 8, :] = jnp.broadcast_to(loss, (8, wide))
    out[rank + 8:rank + 16, :] = jnp.broadcast_to(margin, (8, wide))


def unpack(joined, down_out, up_out, loss_out, margin_out):
    rank, rows = down_out.shape
    up_rows = up_out.shape[0]
    down_out[...] = joined[0:rank, 0:rows]
    up_out[...] = joined[0:up_rows, rows:rows + up_out.shape[1]]
    loss_out[0] = jnp.max(joined[rank:rank + 8, 0:LANES])
    margin_out[0] = jnp.max(joined[rank + 8:rank + 16, 0:LANES])


def shards(n_dp, n_fsdp, hidden_input, readout, response, value_matrix, adapter_down, adapter_up):
    seq = hidden_input.shape[2]
    tokens = 2 * seq
    model = hidden_input.shape[3]
    rows, features = value_matrix.shape
    rank = adapter_down.shape[1]
    half = n_fsdp // 2
    quarter = rank // 4
    wide = rows + LANES
    f32, bf16 = jnp.float32, jnp.bfloat16
    vmem = pl.BlockSpec(memory_space=pltpu.VMEM)
    hbm = pl.BlockSpec(memory_space=pl.ANY)
    dma = pltpu.SemaphoreType.DMA
    joined = pl.pallas_call(
        functools.partial(kernel, n_dp, n_fsdp),
        out_shape=jax.ShapeDtypeStruct((rank + 16, wide), f32),
        in_specs=[hbm, hbm, vmem, hbm, vmem, vmem],
        out_specs=vmem,
        scratch_shapes=[
            pltpu.VMEM((tokens, model), bf16),
            pltpu.VMEM((tokens, features), bf16),
            pltpu.VMEM((tokens, features), f32),
            pltpu.VMEM((n_fsdp, rows + PACK, features), bf16),
            pltpu.VMEM((tokens, features), f32),
            pltpu.VMEM((tokens, LANES), f32),
            pltpu.VMEM((rows, LANES), bf16),
            pltpu.VMEM((rank, tokens), bf16),
            pltpu.VMEM((n_fsdp, 8, LANES), f32),
            pltpu.VMEM((n_fsdp, rank, wide), f32),
            pltpu.VMEM((n_fsdp, rank // 2, wide), f32),
            pltpu.VMEM((n_fsdp, quarter, wide), bf16),
            pltpu.VMEM((n_fsdp, quarter, wide), bf16),
            pltpu.VMEM((n_fsdp, quarter, wide), f32),
            pltpu.VMEM((n_fsdp, quarter, wide), bf16),
            pltpu.VMEM((n_fsdp, quarter, wide), bf16),
            pltpu.VMEM((n_dp, quarter, wide), bf16),
            dma((3,)),
            dma((2, half, 2)), dma((2, half, 2)),
            dma((2, half)), dma((2, half)),
            dma((2, half, 3)), dma((2, half, 3)),
            dma((n_fsdp,)), dma((n_fsdp,)),
            dma((n_fsdp,)), dma((n_fsdp,)),
            dma((n_fsdp,)), dma((n_fsdp,)),
            dma((n_fsdp,)), dma((n_fsdp,)),
            dma((n_dp,)), dma((n_dp,)),
        ],
        compiler_params=pltpu.CompilerParams(
            collective_id=0, has_side_effects=True, vmem_limit_bytes=56 << 20
        ),
        name="dpo_adapter_gradient",
    )(
        hidden_input.reshape(tokens, model),
        readout.reshape(tokens, features),
        response.reshape(2, seq),
        value_matrix,
        adapter_down.T,
        adapter_up,
    )
    smem = pl.BlockSpec(memory_space=pltpu.SMEM)
    down_t, up_block, loss, margin = pl.pallas_call(
        unpack,
        out_shape=(
            jax.ShapeDtypeStruct((rank, rows), f32),
            jax.ShapeDtypeStruct((features // n_fsdp, rank), f32),
            jax.ShapeDtypeStruct((1,), f32),
            jax.ShapeDtypeStruct((1,), f32),
        ),
        in_specs=[vmem],
        out_specs=(vmem, vmem, smem, smem),
        name="unpack_gradients",
    )(joined)
    return down_t.T, up_block, loss, margin


def solution(mesh):
    placed = (
        P("dp", None, "fsdp", None),
        P("dp", None, "fsdp", None),
        P("dp", None, "fsdp"),
        P("fsdp", None),
        P("fsdp", None),
        P(),
    )
    return jax.shard_map(
        functools.partial(shards, mesh.shape["dp"], mesh.shape["fsdp"]),
        mesh=mesh,
        in_specs=placed,
        out_specs=(P("fsdp", None), P("fsdp", None), P("dp"), P("dp")),
        check_vma=False,
    )
```

```python
import functools

import jax
import jax.numpy as jnp
from jax import lax
from jax.experimental import pallas as pl
from jax.experimental.pallas import tpu as pltpu
from jax.sharding import PartitionSpec as P

DPO_BETA = 0.5
ADAPTER_SCALE = 2.0
LANES = 128
PACK = 128
MESH = pl.DeviceIdType.MESH


def kernel(
    n_dp, n_fsdp,
    hid_hbm, read_hbm, resp_ref, value_hbm, down_ref, up_ref,
    out,
    hid, read, weighted, weights, base, acc, spread, grad_low_t,
    ratio_buf, part, buf1, send2, buf2, total2, send3, buf3, final,
    local_sem, ring_s, ring_r, x_s, x_r, core_s, core_r,
    ratio_s, ratio_r, s1, r1, s2, r2, s3, r3, s4, r4,
):
    half = n_fsdp // 2
    rows = value_hbm.shape[0]
    rank = down_ref.shape[0]
    tokens = hid.shape[0]
    seq = tokens // 2
    swapped = weights.shape[1] * 11 // 72 // 16 * 16
    kept = (weights.shape[1] - 4 * swapped) // 2
    groups = rows // PACK
    up_rows = base.shape[1] // n_fsdp

    me = lax.axis_index("fsdp")
    d = lax.axis_index("dp")
    core = lax.rem(d, 2)
    xbit = lax.rem(lax.div(d, 2), 2)
    core_peer = d + 1 - 2 * core
    x_peer = d + 2 - 4 * xbit

    col, row = lax.rem(me, 2), lax.div(me, 2)
    pos = row * (1 - col) + (n_fsdp - 1 - row) * col

    def at(p):
        p = lax.rem(p + 2 * n_fsdp, n_fsdp)
        c = lax.div(p, half)
        r = p * (1 - c) + (n_fsdp - 1 - p) * c
        return 2 * r + c

    ring_peer = (at(pos + 1), at(pos - 1))

    def shard_of(way, s):
        return at(pos - s) if way == 0 else at(pos + s)

    def piece(q, kind, p):
        if kind == 1:
            return weights.at[q, pl.ds(pl.multiple_of(4 * swapped + p * kept, 16), kept), :]
        return weights.at[q, pl.ds(pl.multiple_of(p * swapped, 16), swapped), :]

    own = (xbit * 2 + core, core)
    x_own = (1 - xbit) * 2 + core
    core_own = (xbit * 2 + 1 - core, 1 - core, (1 - xbit) * 2 + 1 - core)

    def remote(src, dst, send, recv, **where):
        return pltpu.make_async_remote_copy(
            src_ref=src, dst_ref=dst, send_sem=send, recv_sem=recv,
            device_id=where, device_id_type=MESH,
        )

    def ring_copy(way, s, kind, q):
        ref = piece(q, kind, own[kind])
        return remote(ref, ref, ring_s.at[way, s - 1, kind], ring_r.at[way, s - 1, kind], fsdp=ring_peer[way])

    def x_copy(way, s, q, p):
        ref = piece(q, 0, p)
        return remote(ref, ref, x_s.at[way, s - 1], x_r.at[way, s - 1], dp=x_peer)

    def core_copy(way, s, kind, q, p):
        ref = piece(q, kind, p)
        return remote(ref, ref, core_s.at[way, s - 1, kind], core_r.at[way, s - 1, kind], dp=core_peer)

    def has(way, s, kind):
        return s < half or (s == half and way == kind)

    value_copy = pltpu.make_async_copy(value_hbm, weights.at[me, pl.ds(0, rows), :], local_sem.at[0])
    hid_copy = pltpu.make_async_copy(hid_hbm, hid, local_sem.at[1])
    read_copy = pltpu.make_async_copy(read_hbm, read, local_sem.at[2])
    value_copy.start()
    hid_copy.start()
    read_copy.start()

    barrier = pltpu.get_barrier_semaphore()

    greeted = [{"fsdp": ring_peer[0]}, {"fsdp": ring_peer[1]}]
    if n_dp == 4:
        greeted += [{"dp": x_peer}, {"dp": core_peer}]
    else:
        greeted += [{"dp": lax.rem(d + k, n_dp)} for k in range(1, n_dp)]
    for where in greeted:
        pl.semaphore_signal(barrier, inc=1, device_id=where, device_id_type=MESH)

    for t in range(groups // 2):
        pair = [down_ref[:, g * PACK:(g + 1) * PACK].astype(jnp.float32) for g in (2 * t, 2 * t + 1)]
        tile = jnp.transpose(jnp.concatenate(pair, axis=0)).astype(jnp.bfloat16)
        weights[me, rows:rows + PACK, t * LANES:(t + 1) * LANES] = tile
    used = groups // 2 * LANES
    if used < weights.shape[2]:
        weights[me, rows:rows + PACK, used:] = jnp.zeros((PACK, weights.shape[2] - used), jnp.bfloat16)

    value_copy.wait()
    pl.semaphore_wait(barrier, len(greeted))

    for kind in (0, 1):
        for way in (0, 1):
            if has(way, 1, kind):
                ring_copy(way, 1, kind, me).start()

    in_left = lax.broadcasted_iota(jnp.int32, (PACK, LANES), 1) < rank

    def multiply(q):
        first = pl.multiple_of(q * rows, rows)
        base[...] += jnp.dot(
            hid[:, pl.ds(first, rows)], weights[q, 0:rows, :], preferred_element_type=jnp.float32
        )
        for t in range(groups // 2):
            tile = weights[q, rows:rows + PACK, t * LANES:(t + 1) * LANES]
            zero = jnp.zeros_like(tile)
            spread[2 * t * PACK:(2 * t + 1) * PACK, :] = jnp.where(in_left, tile, zero)
            spread[(2 * t + 1) * PACK:(2 * t + 2) * PACK, :] = jnp.where(in_left, zero, tile)
        acc[...] += jnp.dot(hid[:, pl.ds(first, rows)], spread[...], preferred_element_type=jnp.float32)

    base[...] = jnp.zeros_like(base)
    acc[...] = jnp.zeros_like(acc)
    hid_copy.wait()
    multiply(me)

    read_copy.wait()
    resp = resp_ref[...].astype(jnp.float32)
    masks = [
        jnp.transpose(jnp.broadcast_to(resp[i:i + 1, :], (seq, seq)))[:, 0:1] for i in (0, 1)
    ]
    weighted[...] = read[...].astype(jnp.float32) * jnp.concatenate(masks, axis=0)

    def take_ring(s, kind):
        for way in (0, 1):
            if has(way, s, kind):
                q = shard_of(way, s)
                ring_copy(way, s, kind, q).wait_recv()
                if has(way, s + 1, kind):
                    ring_copy(way, s + 1, kind, q).start()
                if kind == 0:
                    x_copy(way, s, q, own[0]).start()
                core_copy(way, s, kind, q, own[kind]).start()

    def take_x(s):
        for way in (0, 1):
            if has(way, s, 0):
                q = shard_of(way, s)
                x_copy(way, s, q, x_own).wait_recv()
                core_copy(way, s, 2, q, x_own).start()

    def take_core(way, s):
        for kind in (0, 1, 2):
            if has(way, s, kind % 2):
                core_copy(way, s, kind, shard_of(way, s), core_own[kind]).wait_recv()

    def finish(way, s):
        take_core(way, s)
        multiply(shard_of(way, s))

    for s in range(1, half + 1):
        take_ring(s, 0)
        if s > 1:
            take_x(s - 1)
        take_ring(s, 1)
        if s > 1:
            finish(0, s - 1)
            finish(1, s - 1)
    take_x(half)
    take_core(0, half)
    finish(1, half)

    low = (acc[:, 0:rank] + acc[:, rank:2 * rank]).astype(jnp.bfloat16)
    ref_act = base[...]
    policy = ref_act + ADAPTER_SCALE * jnp.dot(low, up_ref[...], preferred_element_type=jnp.float32)
    t_policy = jnp.tanh(policy)
    scores = weighted[...] * (t_policy - jnp.tanh(ref_act))
    diff = scores[0:seq, :] - scores[seq:, :]
    tile = jnp.zeros((seq, LANES), jnp.float32)
    for t in range(diff.shape[1] // LANES):
        tile += diff[:, t * LANES:(t + 1) * LANES]
    ratio_buf[me] = jnp.sum(tile.reshape(seq // 8, 8, LANES), axis=0)

    def ratio_copy(k):
        return remote(
            ratio_buf.at[me], ratio_buf.at[me], ratio_s.at[k], ratio_r.at[k], fsdp=lax.rem(me + k, n_fsdp)
        )

    def each(first, last, body):
        def step(k, _):
            body(k)
            return 0
        lax.fori_loop(first, last, step, 0)

    each(1, n_fsdp, lambda k: ratio_copy(k).start())
    slope = DPO_BETA * weighted[...] * (1.0 - t_policy * t_policy)
    grad_h = jnp.concatenate([-slope[0:seq, :], slope[seq:, :]], axis=0).astype(jnp.bfloat16)
    grad_low = ADAPTER_SCALE * lax.dot_general(
        grad_h, up_ref[...], (((1,), (1,)), ((), ())), preferred_element_type=jnp.float32
    )
    grad_low_t[...] = jnp.transpose(grad_low).astype(jnp.bfloat16)
    grad_b_t = ADAPTER_SCALE * lax.dot_general(
        grad_h, low, (((0,), (0,)), ((), ())), preferred_element_type=jnp.float32
    )
    for q in range(n_fsdp):
        block = grad_b_t[q * up_rows:(q + 1) * up_rows, :]
        block = jnp.concatenate([block, jnp.zeros((up_rows, LANES - rank), jnp.float32)], axis=1)
        if up_rows < rank:
            block = jnp.concatenate([block, jnp.zeros((rank - up_rows, LANES), jnp.float32)], axis=0)
        part[q, :, rows:rows + LANES] = block

    half_rows, quarter = rank // 2, rank // 4
    mine1 = pl.multiple_of(core * half_rows, half_rows)
    theirs1 = pl.multiple_of((1 - core) * half_rows, half_rows)

    def block_of(k):
        return lax.rem(me + k, n_fsdp)

    def copy1(k):
        return remote(
            part.at[block_of(k), pl.ds(theirs1, half_rows), :], buf1.at[k], s1.at[k], r1.at[k], dp=core_peer
        )

    def copy2(k):
        return remote(send2.at[k], buf2.at[k], s2.at[k], r2.at[k], dp=x_peer)

    def copy3(k):
        return remote(send3.at[k], buf3.at[k], s3.at[k], r3.at[k], fsdp=block_of(k))

    def stage1(k):
        q = block_of(k)
        part[q, :, 0:rows] = jnp.dot(
            grad_low_t[...], hid[:, pl.ds(pl.multiple_of(q * rows, rows), rows)],
            preferred_element_type=jnp.float32,
        )

    def stage2(k):
        q = block_of(k)
        copy1(k).wait_recv()
        give = pl.multiple_of((1 - xbit) * quarter, quarter)
        keep = pl.multiple_of(xbit * quarter, quarter)
        send2[k] = (part[q, pl.ds(mine1 + give, quarter), :] + buf1[k, pl.ds(give, quarter), :]).astype(jnp.bfloat16)
        copy2(k).start()
        total2[k] = part[q, pl.ds(mine1 + keep, quarter), :] + buf1[k, pl.ds(keep, quarter), :]

    def stage3(k):
        copy2(k).wait_recv()
        send3[k] = (total2[k] + buf2[k].astype(jnp.float32)).astype(jnp.bfloat16)
        copy3(k).start()

    def in_order(body, count=n_fsdp, begin=0):
        def step(i):
            odd = lax.rem(i, 2)
            body(half + lax.div(i, 2) * (1 - odd) - lax.div(i + 1, 2) * odd)
        each(begin, count, step)

    in_order(stage1, half)

    each(1, n_fsdp, lambda k: ratio_copy(k).wait())
    margin = DPO_BETA * jnp.sum(jnp.sum(ratio_buf[...], axis=0), keepdims=True)
    loss = jnp.maximum(-margin, 0.0) + jnp.log1p(jnp.exp(-jnp.abs(margin)))
    gate = 1.0 / (1.0 + jnp.exp(margin))

    def send1(k):
        q = block_of(k)
        part[q] = part[q] * gate
        copy1(k).start()

    def both1(k):
        stage1(k)
        send1(k)

    in_order(send1, half)
    in_order(both1, n_fsdp, half)
    in_order(stage2)
    in_order(stage3, n_fsdp - 1)
    copy2(0).wait_recv()
    total2[0] = total2[0] + buf2[0].astype(jnp.float32)

    def stage4(k):
        copy3(k).wait_recv()
        total2[0] = total2[0] + buf3[k].astype(jnp.float32)

    in_order(stage4, n_fsdp - 1)
    final[0] = total2[0].astype(jnp.bfloat16)

    def copy4(k):
        return remote(final.at[0], final.at[k], s4.at[k], r4.at[k], dp=lax.rem(d + k, n_dp))

    each(1, n_dp, lambda k: copy4(k).start())

    for s in range(1, half + 1):
        for way in (0, 1):
            for kind in (0, 1):
                if has(way, s, kind):
                    ring_copy(way, s, kind, me).wait_send()
                    core_copy(way, s, kind, me, own[kind]).wait_send()
            if has(way, s, 0):
                x_copy(way, s, me, own[0]).wait_send()
                core_copy(way, s, 2, me, x_own).wait_send()
    each(0, n_fsdp, lambda k: copy1(k).wait_send())
    each(0, n_fsdp, lambda k: copy2(k).wait_send())
    each(1, n_fsdp, lambda k: copy3(k).wait_send())

    each(1, n_dp, lambda k: copy4(k).wait())
    for c in (0, 1):
        for x in (0, 1):
            begin = c * half_rows + x * quarter
            total = jnp.zeros((quarter, rows + LANES), jnp.float32)
            for h in range(n_dp // 4):
                slot = lax.rem(d - (h * 4 + x * 2 + c) + n_dp, n_dp)
                total += final[slot].astype(jnp.float32)
            out[begin:begin + quarter, :] = total
    wide = rows + LANES
    out[rank:rank + 8, :] = jnp.broadcast_to(loss, (8, wide))
    out[rank + 8:rank + 16, :] = jnp.broadcast_to(margin, (8, wide))


def unpack(joined, down_out, up_out, loss_out, margin_out):
    rank, rows = down_out.shape
    up_rows = up_out.shape[0]
    down_out[...] = joined[0:rank, 0:rows]
    up_out[...] = joined[0:up_rows, rows:rows + up_out.shape[1]]
    loss_out[0] = jnp.max(joined[rank:rank + 8, 0:LANES])
    margin_out[0] = jnp.max(joined[rank + 8:rank + 16, 0:LANES])


def shards(n_dp, n_fsdp, hidden_input, readout, response, value_matrix, adapter_down, adapter_up):
    seq = hidden_input.shape[2]
    tokens = 2 * seq
    model = hidden_input.shape[3]
    rows, features = value_matrix.shape
    rank = adapter_down.shape[1]
    half = n_fsdp // 2
    quarter = rank // 4
    wide = rows + LANES
    f32, bf16 = jnp.float32, jnp.bfloat16
    vmem = pl.BlockSpec(memory_space=pltpu.VMEM)
    hbm = pl.BlockSpec(memory_space=pl.ANY)
    dma = pltpu.SemaphoreType.DMA
    joined = pl.pallas_call(
        functools.partial(kernel, n_dp, n_fsdp),
        out_shape=jax.ShapeDtypeStruct((rank + 16, wide), f32),
        in_specs=[hbm, hbm, vmem, hbm, vmem, vmem],
        out_specs=vmem,
        scratch_shapes=[
            pltpu.VMEM((tokens, model), bf16),
            pltpu.VMEM((tokens, features), bf16),
            pltpu.VMEM((tokens, features), f32),
            pltpu.VMEM((n_fsdp, rows + PACK, features), bf16),
            pltpu.VMEM((tokens, features), f32),
            pltpu.VMEM((tokens, LANES), f32),
            pltpu.VMEM((rows, LANES), bf16),
            pltpu.VMEM((rank, tokens), bf16),
            pltpu.VMEM((n_fsdp, 8, LANES), f32),
            pltpu.VMEM((n_fsdp, rank, wide), f32),
            pltpu.VMEM((n_fsdp, rank // 2, wide), f32),
            pltpu.VMEM((n_fsdp, quarter, wide), bf16),
            pltpu.VMEM((n_fsdp, quarter, wide), bf16),
            pltpu.VMEM((n_fsdp, quarter, wide), f32),
            pltpu.VMEM((n_fsdp, quarter, wide), bf16),
            pltpu.VMEM((n_fsdp, quarter, wide), bf16),
            pltpu.VMEM((n_dp, quarter, wide), bf16),
            dma((3,)),
            dma((2, half, 2)), dma((2, half, 2)),
            dma((2, half)), dma((2, half)),
            dma((2, half, 3)), dma((2, half, 3)),
            dma((n_fsdp,)), dma((n_fsdp,)),
            dma((n_fsdp,)), dma((n_fsdp,)),
            dma((n_fsdp,)), dma((n_fsdp,)),
            dma((n_fsdp,)), dma((n_fsdp,)),
            dma((n_dp,)), dma((n_dp,)),
        ],
        compiler_params=pltpu.CompilerParams(
            collective_id=0, has_side_effects=True, vmem_limit_bytes=56 << 20
        ),
        name="dpo_adapter_gradient",
    )(
        hidden_input.reshape(tokens, model),
        readout.reshape(tokens, features),
        response.reshape(2, seq),
        value_matrix,
        adapter_down.T,
        adapter_up,
    )
    smem = pl.BlockSpec(memory_space=pltpu.SMEM)
    down_t, up_block, loss, margin = pl.pallas_call(
        unpack,
        out_shape=(
            jax.ShapeDtypeStruct((rank, rows), f32),
            jax.ShapeDtypeStruct((features // n_fsdp, rank), f32),
            jax.ShapeDtypeStruct((1,), f32),
            jax.ShapeDtypeStruct((1,), f32),
        ),
        in_specs=[vmem],
        out_specs=(vmem, vmem, smem, smem),
        name="unpack_gradients",
    )(joined)
    return down_t.T, up_block, loss, margin


def solution(mesh):
    placed = (
        P("dp", None, "fsdp", None),
        P("dp", None, "fsdp", None),
        P("dp", None, "fsdp"),
        P("fsdp", None),
        P("fsdp", None),
        P(),
    )
    return jax.shard_map(
        functools.partial(shards, mesh.shape["dp"], mesh.shape["fsdp"]),
        mesh=mesh,
        in_specs=placed,
        out_specs=(P("fsdp", None), P("fsdp", None), P("dp"), P("dp")),
        check_vma=False,
    )
```

```python
import functools

import jax
import jax.numpy as jnp
from jax import lax
from jax.experimental import pallas as pl
from jax.experimental.pallas import tpu as pltpu
from jax.sharding import PartitionSpec as P

DPO_BETA = 0.5
ADAPTER_SCALE = 2.0
LANES = 128
PACK = 128
MESH = pl.DeviceIdType.MESH


def kernel(
    n_dp, n_fsdp,
    hid_hbm, read_hbm, resp_ref, value_hbm, down_ref, up_ref,
    out,
    hid, read, weighted, weights, base, acc, spread, grad_low_t,
    ratio_buf, part, buf1, send2, buf2, total2, send3, buf3, final,
    local_sem, ring_s, ring_r, x_s, x_r, core_s, core_r,
    first_s, first_r, first_xs, first_xr,
    ratio_s, ratio_r, s1, r1, s2, r2, s3, r3, s4, r4,
):
    half = n_fsdp // 2
    rows = value_hbm.shape[0]
    rank = down_ref.shape[0]
    tokens = hid.shape[0]
    seq = tokens // 2
    swapped = weights.shape[1] * 11 // 72 // 16 * 16
    kept = (weights.shape[1] - 4 * swapped) // 2
    groups = rows // PACK
    up_rows = base.shape[1] // n_fsdp

    me = lax.axis_index("fsdp")
    d = lax.axis_index("dp")
    core = lax.rem(d, 2)
    xbit = lax.rem(lax.div(d, 2), 2)
    core_peer = d + 1 - 2 * core
    x_peer = d + 2 - 4 * xbit

    col, row = lax.rem(me, 2), lax.div(me, 2)
    pos = row * (1 - col) + (n_fsdp - 1 - row) * col

    def at(p):
        p = lax.rem(p + 2 * n_fsdp, n_fsdp)
        c = lax.div(p, half)
        r = p * (1 - c) + (n_fsdp - 1 - p) * c
        return 2 * r + c

    ring_peer = (at(pos + 1), at(pos - 1))

    def shard_of(way, s):
        return at(pos - s) if way == 0 else at(pos + s)

    def piece(q, kind, p):
        if kind == 1:
            return weights.at[q, pl.ds(pl.multiple_of(4 * swapped + p * kept, 16), kept), :]
        return weights.at[q, pl.ds(pl.multiple_of(p * swapped, 16), swapped), :]

    own = (xbit * 2 + core, core)
    x_own = (1 - xbit) * 2 + core
    core_own = (xbit * 2 + 1 - core, 1 - core, (1 - xbit) * 2 + 1 - core)

    def remote(src, dst, send, recv, **where):
        return pltpu.make_async_remote_copy(
            src_ref=src, dst_ref=dst, send_sem=send, recv_sem=recv,
            device_id=where, device_id_type=MESH,
        )

    def ring_copy(way, s, kind, q):
        ref = piece(q, kind, own[kind])
        return remote(ref, ref, ring_s.at[way, s - 1, kind], ring_r.at[way, s - 1, kind], fsdp=ring_peer[way])

    def x_copy(way, s, q, p):
        ref = piece(q, 0, p)
        return remote(ref, ref, x_s.at[way, s - 1], x_r.at[way, s - 1], dp=x_peer)

    def core_copy(way, s, kind, q, p):
        ref = piece(q, kind, p)
        return remote(ref, ref, core_s.at[way, s - 1, kind], core_r.at[way, s - 1, kind], dp=core_peer)

    cut = (swapped // 2 + 15) // 16 * 16

    def part_of(q, p, h):
        begin = pl.multiple_of(p * swapped + h * cut, 16)
        return weights.at[q, pl.ds(begin, swapped - cut if h else cut), :]

    def first_ring(way, h, q):
        ref = part_of(q, own[0], h)
        return remote(ref, ref, first_s.at[way, h], first_r.at[way, h], fsdp=ring_peer[way])

    def first_x(way, h, q, p):
        ref = part_of(q, p, h)
        return remote(ref, ref, first_xs.at[way, h], first_xr.at[way, h], dp=x_peer)

    def has(way, s, kind):
        return s < half or (s == half and way == kind)

    value_copy = pltpu.make_async_copy(value_hbm, weights.at[me, pl.ds(0, rows), :], local_sem.at[0])
    hid_copy = pltpu.make_async_copy(hid_hbm, hid, local_sem.at[1])
    read_copy = pltpu.make_async_copy(read_hbm, read, local_sem.at[2])
    value_copy.start()
    hid_copy.start()
    read_copy.start()

    barrier = pltpu.get_barrier_semaphore()

    greeted = [{"fsdp": ring_peer[0]}, {"fsdp": ring_peer[1]}]
    if n_dp == 4:
        greeted += [{"dp": x_peer}, {"dp": core_peer}]
    else:
        greeted += [{"dp": lax.rem(d + k, n_dp)} for k in range(1, n_dp)]
    for where in greeted:
        pl.semaphore_signal(barrier, inc=1, device_id=where, device_id_type=MESH)

    for t in range(groups // 2):
        pair = [down_ref[:, g * PACK:(g + 1) * PACK].astype(jnp.float32) for g in (2 * t, 2 * t + 1)]
        tile = jnp.transpose(jnp.concatenate(pair, axis=0)).astype(jnp.bfloat16)
        weights[me, rows:rows + PACK, t * LANES:(t + 1) * LANES] = tile
    used = groups // 2 * LANES
    if used < weights.shape[2]:
        weights[me, rows:rows + PACK, used:] = jnp.zeros((PACK, weights.shape[2] - used), jnp.bfloat16)

    value_copy.wait()
    pl.semaphore_wait(barrier, len(greeted))

    for h in (0, 1):
        for way in (0, 1):
            first_ring(way, h, me).start()
    for way in (0, 1):
        ring_copy(way, 1, 1, me).start()

    in_left = lax.broadcasted_iota(jnp.int32, (PACK, LANES), 1) < rank

    def multiply(q):
        first = pl.multiple_of(q * rows, rows)
        base[...] += jnp.dot(
            hid[:, pl.ds(first, rows)], weights[q, 0:rows, :], preferred_element_type=jnp.float32
        )
        for t in range(groups // 2):
            tile = weights[q, rows:rows + PACK, t * LANES:(t + 1) * LANES]
            zero = jnp.zeros_like(tile)
            spread[2 * t * PACK:(2 * t + 1) * PACK, :] = jnp.where(in_left, tile, zero)
            spread[(2 * t + 1) * PACK:(2 * t + 2) * PACK, :] = jnp.where(in_left, zero, tile)
        acc[...] += jnp.dot(hid[:, pl.ds(first, rows)], spread[...], preferred_element_type=jnp.float32)

    base[...] = jnp.zeros_like(base)
    acc[...] = jnp.zeros_like(acc)
    hid_copy.wait()
    multiply(me)

    read_copy.wait()
    resp = resp_ref[...].astype(jnp.float32)
    masks = [
        jnp.transpose(jnp.broadcast_to(resp[i:i + 1, :], (seq, seq)))[:, 0:1] for i in (0, 1)
    ]
    weighted[...] = read[...].astype(jnp.float32) * jnp.concatenate(masks, axis=0)

    def take_first():
        for h in (0, 1):
            for way in (0, 1):
                q = shard_of(way, 1)
                first_ring(way, h, q).wait_recv()
                first_x(way, h, q, own[0]).start()
        for way in (0, 1):
            q = shard_of(way, 1)
            if has(way, 2, 0):
                ring_copy(way, 2, 0, q).start()
            core_copy(way, 1, 0, q, own[0]).start()

    def take_ring(s, kind):
        if s == 1 and kind == 0:
            take_first()
            return
        for way in (0, 1):
            if has(way, s, kind):
                q = shard_of(way, s)
                ring_copy(way, s, kind, q).wait_recv()
                if has(way, s + 1, kind):
                    ring_copy(way, s + 1, kind, q).start()
                if kind == 0:
                    x_copy(way, s, q, own[0]).start()
                core_copy(way, s, kind, q, own[kind]).start()

    def take_x(s):
        for way in (0, 1):
            if has(way, s, 0):
                q = shard_of(way, s)
                if s == 1:
                    first_x(way, 0, q, x_own).wait_recv()
                    first_x(way, 1, q, x_own).wait_recv()
                else:
                    x_copy(way, s, q, x_own).wait_recv()
                core_copy(way, s, 2, q, x_own).start()

    def take_core(way, s):
        for kind in (0, 1, 2):
            if has(way, s, kind % 2):
                core_copy(way, s, kind, shard_of(way, s), core_own[kind]).wait_recv()

    def finish(way, s):
        take_core(way, s)
        multiply(shard_of(way, s))

    for s in range(1, half + 1):
        take_ring(s, 0)
        if s > 1:
            take_x(s - 1)
        take_ring(s, 1)
        if s > 1:
            finish(0, s - 1)
            finish(1, s - 1)
    take_x(half)
    take_core(0, half)
    finish(1, half)

    low = (acc[:, 0:rank] + acc[:, rank:2 * rank]).astype(jnp.bfloat16)
    ref_act = base[...]
    policy = ref_act + ADAPTER_SCALE * jnp.dot(low, up_ref[...], preferred_element_type=jnp.float32)
    t_policy = jnp.tanh(policy)
    scores = weighted[...] * (t_policy - jnp.tanh(ref_act))
    diff = scores[0:seq, :] - scores[seq:, :]
    tile = jnp.zeros((seq, LANES), jnp.float32)
    for t in range(diff.shape[1] // LANES):
        tile += diff[:, t * LANES:(t + 1) * LANES]
    ratio_buf[me] = jnp.sum(tile.reshape(seq // 8, 8, LANES), axis=0)

    def ratio_copy(k):
        return remote(
            ratio_buf.at[me], ratio_buf.at[me], ratio_s.at[k], ratio_r.at[k], fsdp=lax.rem(me + k, n_fsdp)
        )

    def each(first, last, body):
        def step(k, _):
            body(k)
            return 0
        lax.fori_loop(first, last, step, 0)

    each(1, n_fsdp, lambda k: ratio_copy(k).start())
    slope = DPO_BETA * weighted[...] * (1.0 - t_policy * t_policy)
    grad_h = jnp.concatenate([-slope[0:seq, :], slope[seq:, :]], axis=0).astype(jnp.bfloat16)
    grad_low = ADAPTER_SCALE * lax.dot_general(
        grad_h, up_ref[...], (((1,), (1,)), ((), ())), preferred_element_type=jnp.float32
    )
    grad_low_t[...] = jnp.transpose(grad_low).astype(jnp.bfloat16)
    grad_b_t = ADAPTER_SCALE * lax.dot_general(
        grad_h, low, (((0,), (0,)), ((), ())), preferred_element_type=jnp.float32
    )
    for q in range(n_fsdp):
        block = grad_b_t[q * up_rows:(q + 1) * up_rows, :]
        block = jnp.concatenate([block, jnp.zeros((up_rows, LANES - rank), jnp.float32)], axis=1)
        if up_rows < rank:
            block = jnp.concatenate([block, jnp.zeros((rank - up_rows, LANES), jnp.float32)], axis=0)
        part[q, :, rows:rows + LANES] = block

    half_rows, quarter = rank // 2, rank // 4
    mine1 = pl.multiple_of(core * half_rows, half_rows)
    theirs1 = pl.multiple_of((1 - core) * half_rows, half_rows)

    def block_of(k):
        return lax.rem(me + k, n_fsdp)

    def copy1(k):
        return remote(
            part.at[block_of(k), pl.ds(theirs1, half_rows), :], buf1.at[k], s1.at[k], r1.at[k], dp=core_peer
        )

    def copy2(k):
        return remote(send2.at[k], buf2.at[k], s2.at[k], r2.at[k], dp=x_peer)

    def copy3(k):
        return remote(send3.at[k], buf3.at[k], s3.at[k], r3.at[k], fsdp=block_of(k))

    def stage1(k):
        q = block_of(k)
        part[q, :, 0:rows] = jnp.dot(
            grad_low_t[...], hid[:, pl.ds(pl.multiple_of(q * rows, rows), rows)],
            preferred_element_type=jnp.float32,
        )

    def stage2(k):
        q = block_of(k)
        copy1(k).wait_recv()
        give = pl.multiple_of((1 - xbit) * quarter, quarter)
        keep = pl.multiple_of(xbit * quarter, quarter)
        send2[k] = (part[q, pl.ds(mine1 + give, quarter), :] + buf1[k, pl.ds(give, quarter), :]).astype(jnp.bfloat16)
        copy2(k).start()
        total2[k] = part[q, pl.ds(mine1 + keep, quarter), :] + buf1[k, pl.ds(keep, quarter), :]

    def stage3(k):
        copy2(k).wait_recv()
        send3[k] = (total2[k] + buf2[k].astype(jnp.float32)).astype(jnp.bfloat16)
        copy3(k).start()

    def in_order(body, count=n_fsdp, begin=0):
        def step(i):
            odd = lax.rem(i, 2)
            body(half + lax.div(i, 2) * (1 - odd) - lax.div(i + 1, 2) * odd)
        each(begin, count, step)

    in_order(stage1, half)

    each(1, n_fsdp, lambda k: ratio_copy(k).wait())
    margin = DPO_BETA * jnp.sum(jnp.sum(ratio_buf[...], axis=0), keepdims=True)
    loss = jnp.maximum(-margin, 0.0) + jnp.log1p(jnp.exp(-jnp.abs(margin)))
    gate = 1.0 / (1.0 + jnp.exp(margin))

    def send1(k):
        q = block_of(k)
        part[q] = part[q] * gate
        copy1(k).start()

    def both1(k):
        stage1(k)
        send1(k)

    in_order(send1, half)
    in_order(both1, n_fsdp, half)
    in_order(stage2)
    in_order(stage3, n_fsdp - 1)
    copy2(0).wait_recv()
    total2[0] = total2[0] + buf2[0].astype(jnp.float32)

    def stage4(k):
        copy3(k).wait_recv()
        total2[0] = total2[0] + buf3[k].astype(jnp.float32)

    in_order(stage4, n_fsdp - 1)
    final[0] = total2[0].astype(jnp.bfloat16)

    def copy4(k):
        return remote(final.at[0], final.at[k], s4.at[k], r4.at[k], dp=lax.rem(d + k, n_dp))

    each(1, n_dp, lambda k: copy4(k).start())

    for s in range(1, half + 1):
        for way in (0, 1):
            for kind in (0, 1):
                if has(way, s, kind):
                    if s == 1 and kind == 0:
                        for h in (0, 1):
                            first_ring(way, h, me).wait_send()
                            first_x(way, h, me, own[0]).wait_send()
                    else:
                        ring_copy(way, s, kind, me).wait_send()
                    core_copy(way, s, kind, me, own[kind]).wait_send()
            if has(way, s, 0):
                if s > 1:
                    x_copy(way, s, me, own[0]).wait_send()
                core_copy(way, s, 2, me, x_own).wait_send()
    each(0, n_fsdp, lambda k: copy1(k).wait_send())
    each(0, n_fsdp, lambda k: copy2(k).wait_send())
    each(1, n_fsdp, lambda k: copy3(k).wait_send())

    each(1, n_dp, lambda k: copy4(k).wait())
    for c in (0, 1):
        for x in (0, 1):
            begin = c * half_rows + x * quarter
            total = jnp.zeros((quarter, rows + LANES), jnp.float32)
            for h in range(n_dp // 4):
                slot = lax.rem(d - (h * 4 + x * 2 + c) + n_dp, n_dp)
                total += final[slot].astype(jnp.float32)
            out[begin:begin + quarter, :] = total
    wide = rows + LANES
    out[rank:rank + 8, :] = jnp.broadcast_to(loss, (8, wide))
    out[rank + 8:rank + 16, :] = jnp.broadcast_to(margin, (8, wide))


def unpack(joined, down_out, up_out, loss_out, margin_out):
    rank, rows = down_out.shape
    up_rows = up_out.shape[0]
    down_out[...] = joined[0:rank, 0:rows]
    up_out[...] = joined[0:up_rows, rows:rows + up_out.shape[1]]
    loss_out[0] = jnp.max(joined[rank:rank + 8, 0:LANES])
    margin_out[0] = jnp.max(joined[rank + 8:rank + 16, 0:LANES])


def shards(n_dp, n_fsdp, hidden_input, readout, response, value_matrix, adapter_down, adapter_up):
    seq = hidden_input.shape[2]
    tokens = 2 * seq
    model = hidden_input.shape[3]
    rows, features = value_matrix.shape
    rank = adapter_down.shape[1]
    half = n_fsdp // 2
    quarter = rank // 4
    wide = rows + LANES
    f32, bf16 = jnp.float32, jnp.bfloat16
    vmem = pl.BlockSpec(memory_space=pltpu.VMEM)
    hbm = pl.BlockSpec(memory_space=pl.ANY)
    dma = pltpu.SemaphoreType.DMA
    joined = pl.pallas_call(
        functools.partial(kernel, n_dp, n_fsdp),
        out_shape=jax.ShapeDtypeStruct((rank + 16, wide), f32),
        in_specs=[hbm, hbm, vmem, hbm, vmem, vmem],
        out_specs=vmem,
        scratch_shapes=[
            pltpu.VMEM((tokens, model), bf16),
            pltpu.VMEM((tokens, features), bf16),
            pltpu.VMEM((tokens, features), f32),
            pltpu.VMEM((n_fsdp, rows + PACK, features), bf16),
            pltpu.VMEM((tokens, features), f32),
            pltpu.VMEM((tokens, LANES), f32),
            pltpu.VMEM((rows, LANES), bf16),
            pltpu.VMEM((rank, tokens), bf16),
            pltpu.VMEM((n_fsdp, 8, LANES), f32),
            pltpu.VMEM((n_fsdp, rank, wide), f32),
            pltpu.VMEM((n_fsdp, rank // 2, wide), f32),
            pltpu.VMEM((n_fsdp, quarter, wide), bf16),
            pltpu.VMEM((n_fsdp, quarter, wide), bf16),
            pltpu.VMEM((n_fsdp, quarter, wide), f32),
            pltpu.VMEM((n_fsdp, quarter, wide), bf16),
            pltpu.VMEM((n_fsdp, quarter, wide), bf16),
            pltpu.VMEM((n_dp, quarter, wide), bf16),
            dma((3,)),
            dma((2, half, 2)), dma((2, half, 2)),
            dma((2, half)), dma((2, half)),
            dma((2, half, 3)), dma((2, half, 3)),
            dma((2, 2)), dma((2, 2)), dma((2, 2)), dma((2, 2)),
            dma((n_fsdp,)), dma((n_fsdp,)),
            dma((n_fsdp,)), dma((n_fsdp,)),
            dma((n_fsdp,)), dma((n_fsdp,)),
            dma((n_fsdp,)), dma((n_fsdp,)),
            dma((n_dp,)), dma((n_dp,)),
        ],
        compiler_params=pltpu.CompilerParams(
            collective_id=0, has_side_effects=True, vmem_limit_bytes=56 << 20
        ),
        name="dpo_adapter_gradient",
    )(
        hidden_input.reshape(tokens, model),
        readout.reshape(tokens, features),
        response.reshape(2, seq),
        value_matrix,
        adapter_down.T,
        adapter_up,
    )
    smem = pl.BlockSpec(memory_space=pltpu.SMEM)
    down_t, up_block, loss, margin = pl.pallas_call(
        unpack,
        out_shape=(
            jax.ShapeDtypeStruct((rank, rows), f32),
            jax.ShapeDtypeStruct((features // n_fsdp, rank), f32),
            jax.ShapeDtypeStruct((1,), f32),
            jax.ShapeDtypeStruct((1,), f32),
        ),
        in_specs=[vmem],
        out_specs=(vmem, vmem, smem, smem),
        name="unpack_gradients",
    )(joined)
    return down_t.T, up_block, loss, margin


def solution(mesh):
    placed = (
        P("dp", None, "fsdp", None),
        P("dp", None, "fsdp", None),
        P("dp", None, "fsdp"),
        P("fsdp", None),
        P("fsdp", None),
        P(),
    )
    return jax.shard_map(
        functools.partial(shards, mesh.shape["dp"], mesh.shape["fsdp"]),
        mesh=mesh,
        in_specs=placed,
        out_specs=(P("fsdp", None), P("fsdp", None), P("dp"), P("dp")),
        check_vma=False,
    )
```
